32 devices in a mesh: design: 2 (over y), brick: 4 (over z), case: 2 (over x), sub: 2 (over core).
Axes of the slice: x: 2, y: 2, z: 4, core: 2. Of those that a mesh axis runs over, the one named last changes fastest.
Arguments:
- densities: float32 [64, 16, 128], P(('design', 'brick'), 'sub'), parts along dimension 0, may hold values from 0.1 to 1
- fixed_mask: int32 [3, 64, 16, 128], P(None, ('design', 'brick'), 'sub'), parts along dimension 1, may hold values 0 or 1
- start_field: float32 [8, 3, 64, 16, 128], P('case', None, ('design', 'brick'), 'sub'), parts along dimension 2, may hold values from -2.4 to 2.4
- load_nodes: int32 [8, 64], P('case'), may hold values from 0 to 65535
- load_forces: int32 [8, 64, 3], P('case'), may hold values from -4 to 4
- case_weights: int32 [8], replicated, may hold values from 1 to 4
- stiffness: float32 [24, 24], replicated, may hold values from -0.05 to 2, as said below
Outputs:
- displacement: float32 [8, 3, 64, 16, 128], P('case', None, ('design', 'brick'), 'sub'), parts along dimension 2
- sensitivity: float32 [64, 16, 128], P(('design', 'brick'), 'sub', 'case'), parts along dimension 0
The draws below stay inside these ranges and needn't reach their ends.
There are 2 independent parts, one for each index of `design`. The reference program is written for one: setup_inputs(seed, part) draws one part's arguments, and reference() takes and returns one part's arrays. A program takes and returns all parts, laid end to end along the dimension named above; an argument that names none is the same for every part. Nothing has to cross between parts.
Inputs may be any that keep to these rules, and one draw needn't show every extreme that they name: `stiffness`: symmetric; each diagonal entry exceeds the sum of magnitudes of the other entries of its row.
All inputs are finite; a program needn't handle non-finite values. No bound on the sum of `fixed_mask` on one device may be relied on, other than what follows from the above.
Results may differ from the reference program's by a relative error of at most 0.00023.
Values sent between devices are 32-bit elements; how exact they have to be, the bound alone decides.
A program may use at most 128 MiB of HBM per device.

```python
import jax
import jax.numpy as jnp
from jax import lax

LZ = 128
CASES = 8
LOADS = 64
ITERS = 2
NX = 32
NY = 16


def draw_stiffness(key, part):
    key = jax.random.fold_in(key, 7)
    first, second = jax.random.split(key)
    offdiag = jax.random.uniform(first, (24, 24), jnp.float32, -1.0, 1.0) / 23.0
    offdiag = 0.5 * (offdiag + offdiag.T)
    identity = jnp.eye(24, dtype=jnp.float32)
    diagonal = jax.random.uniform(second, (24,), jnp.float32, 1.05, 2.0)
    return offdiag * (1.0 - identity) + diagonal[None, :] * identity


def touch_ends(entries, rng, smallest, largest):
    extent = entries.shape
    place = [jax.random.randint(jax.random.fold_in(rng, axis), (), 0, extent[axis]) for axis in range(len(extent))]
    entries = entries.at[tuple(place)].set(smallest)
    longest = extent.index(max(extent))
    place[longest] = (place[longest] + 1) % extent[longest]
    return entries.at[tuple(place)].set(largest)


def levels(own_key, extent, cuts, low, top_value):
    factor_of = 1.0
    for dim, parts in cuts:
        draws = jax.random.uniform(jax.random.fold_in(jax.random.fold_in(own_key, 6), dim), (parts,), jnp.float32, low / len(cuts), top_value / len(cuts))
        factor_of = factor_of * jnp.repeat(jnp.exp(draws), extent[dim] // parts).reshape((-1,) + (1,) * (len(extent) - 1 - dim))
    return factor_of


def scatter_about(rng, extent, spread, most, pieces=(), kind=jnp.bfloat16):
    result = spread * jax.random.normal(rng, extent, jnp.float32)
    if pieces:
        result = result * levels(rng, extent, pieces, -0.22, 0.18)
    return jnp.clip(result, -most, most).astype(kind)


def setup_inputs(seed: int = 0, part: int = 0) -> dict:
    arg_keys = jax.random.split(jax.random.key(seed), 8)
    part_splits = jax.random.split(jax.random.fold_in(arg_keys[7], part), 8)
    densities = jnp.clip(0.1 + 0.9 * jax.random.uniform(part_splits[0], (NX, NY, LZ), jnp.float32) ** levels(part_splits[0], (NX, NY, LZ), ((0, 4), (1, 2)), -0.2, 0.2), 0.1, 1.0)
    fixed_mask = touch_ends((jax.random.randint(part_splits[1], (3, NX, NY, LZ), 0, 8) < 1).astype(jnp.int32), jax.random.fold_in(part_splits[1], 1), 0, 1)
    start_field = scatter_about(part_splits[2], (CASES, 3, NX, NY, LZ), 0.3, 2.4, ((0, 2), (2, 4), (3, 2)), jnp.float32)
    load_nodes = touch_ends(jax.random.randint(arg_keys[3], (CASES, LOADS), 0, NX * NY * LZ), jax.random.fold_in(arg_keys[3], 1), 0, (NX * NY * LZ) - 1).astype(jnp.int32)
    load_forces = touch_ends(jax.random.randint(arg_keys[4], (CASES, LOADS, 3), -4, 5), jax.random.fold_in(arg_keys[4], 1), -4, 4).astype(jnp.int32)
    case_weights = touch_ends(jax.random.randint(arg_keys[5], (CASES,), 1, 5), jax.random.fold_in(arg_keys[5], 1), 1, 4).astype(jnp.int32)
    stiffness = draw_stiffness(jax.random.fold_in(arg_keys[7], 71), part)
    return {"densities": densities, "fixed_mask": fixed_mask, "start_field": start_field, "load_nodes": load_nodes, "load_forces": load_forces, "case_weights": case_weights, "stiffness": stiffness}


PENALTY = 3.0
SOFT_FLOOR = 0.001
CORNERS = [(a, b, c) for a in (0, 1) for b in (0, 1) for c in (0, 1)]


def element_terms(window, stiffness):
    cells_x = window.shape[2] - 1
    cells_y = window.shape[3] - 1
    cells_z = window.shape[4]
    padded = jnp.pad(window, ((0, 0), (0, 0), (0, 0), (0, 0), (0, 1)))
    stacked = jnp.concatenate([padded[:, :, a:a + cells_x, b:b + cells_y, c:c + cells_z] for (a, b, c) in CORNERS], axis=1)
    unscaled = jnp.einsum('ij,cjxyz->cixyz', stiffness, stacked, precision=lax.Precision.HIGHEST)
    return stacked, unscaled


def assemble(forces, cells_z):
    summed = jnp.zeros((forces.shape[0], 3, forces.shape[2] + 1, forces.shape[3] + 1, cells_z), jnp.float32)
    for k, (a, b, c) in enumerate(CORNERS):
        corner_part = forces[:, 3 * k:3 * k + 3]
        corner_part = jnp.pad(corner_part, ((0, 0), (0, 0), (a, 1 - a), (b, 1 - b), (c, 0)))[..., :cells_z]
        summed = summed + corner_part
    return summed


def reference(densities, fixed_mask, start_field, load_nodes, load_forces, case_weights, stiffness):
    free_mask = (1 - fixed_mask).astype(jnp.float32)
    element_scale = SOFT_FLOOR + (1.0 - SOFT_FLOOR) * densities ** PENALTY

    def element_pass(field):
        window = jnp.pad(field, ((0, 0), (0, 0), (0, 1), (0, 1), (0, 0)))
        stacked, unscaled = element_terms(window, stiffness)
        node_forces = assemble(unscaled * element_scale, LZ)[:, :, :NX, :NY]
        return node_forces * free_mask, jnp.sum(stacked * unscaled, axis=1)

    def solve_case(operands):
        targets, forces, start = operands
        right_side = jnp.zeros((3, NX * NY * LZ), jnp.float32).at[:, targets].add(forces.T.astype(jnp.float32))
        right_side = right_side.reshape(3, NX, NY, LZ) * free_mask
        displace = (start * free_mask)[None]
        residual = right_side[None] - element_pass(displace)[0]
        direction = residual
        norm_now = jnp.sum(residual * residual)
        for iteration in range(ITERS):
            image = element_pass(direction)[0]
            step_length = norm_now / jnp.sum(direction * image)
            displace = displace + step_length * direction
            residual = residual - step_length * image
            norm_next = jnp.sum(residual * residual)
            direction = residual + (norm_next / norm_now) * direction
            norm_now = norm_next
        energy = element_pass(displace)[1]
        return displace[0], energy[0]

    fields, energies = lax.map(solve_case, (load_nodes, load_forces, start_field))
    weights = case_weights.astype(jnp.float32)
    weighted = jnp.sum(weights[:, None, None, None] * energies, axis=0)
    sensitivity = -(PENALTY * (1.0 - SOFT_FLOOR)) * densities ** (PENALTY - 1.0) * weighted / jnp.sum(weights)
    return fields, sensitivity
```

```python
import functools

import jax
import jax.numpy as jnp
import numpy as np
from jax import lax
from jax.experimental import pallas as pl
from jax.experimental.pallas import tpu as pltpu
from jax.sharding import PartitionSpec as P

PENALTY = 3.0
SOFT_FLOOR = 0.001
MESH = pl.DeviceIdType.MESH
ROWS = 8
LANES = 128


def corner_index(a, b, c, comp):
    return 3 * (4 * a + 2 * b + c) + comp


def force_constants():
    pick = np.zeros((2, 96, 24), np.float32)
    spread = np.zeros((2, 24, 224), np.float32)
    keep = np.zeros((2, 2, 96, 224), np.float32)
    rows = []
    for a in (0, 1):
        for c in (0, 1):
            for comp in range(3):
                for y in range(ROWS):
                    for b in (0, 1):
                        pick[b, len(rows), corner_index(a, b, c, comp)] = 1
                    rows.append(y)
    for side in (0, 1):
        columns = []
        for a in (0, 1):
            for b in (0, 1):
                for c in (0, 1):
                    for comp in range(3):
                        for y in range(ROWS):
                            columns.append((corner_index(a, b, c, comp), y - b))
            for c in (0, 1):
                for comp in range(ROWS):
                    if comp < 3:
                        b = 1 - side
                        columns.append((corner_index(a, b, c, comp), 7 if side == 0 else -1))
                    else:
                        columns.append(None)
        for n, column in enumerate(columns):
            if column is None:
                continue
            spread[side, column[0], n] = 1
            for m, y in enumerate(rows):
                if y - column[1] in (0, 1):
                    keep[side, y - column[1], m, n] = 1
    return pick, spread, keep


def energy_constants():
    pick = np.zeros((192, 24), np.float32)
    spread = np.zeros((2, 24, 128), np.float32)
    keep = np.zeros((2, 2, 192, 128), np.float32)
    for j in range(24):
        pick[8 * j : 8 * j + 8, j] = 1
    for side in (0, 1):
        for a in (0, 1):
            for c in (0, 1):
                for comp in range(3):
                    for b in (0, 1):
                        for y in range(ROWS):
                            n = 64 * a + 24 * c + 8 * comp + y
                            spread[b, corner_index(a, b, c, comp), n] = 1
                            if y - b >= 0:
                                keep[side, b, y - b :: 8, n] = 1
                        n = 64 * a + 48 + 8 * c + comp
                        spread[b, corner_index(a, b, c, comp), n] = 1
                        if side == 0 and b == 1:
                            keep[side, b, 7::8, n] = 1
    return pick, spread, keep


def split(value):
    high = value.astype(jnp.bfloat16)
    return high, (value - high.astype(jnp.float32)).astype(jnp.bfloat16)


def exact_dot(a, b):
    return jnp.dot(a, b, precision=lax.Precision.HIGHEST, preferred_element_type=jnp.float32)


def dot16(a, b):
    return jnp.dot(a, b, preferred_element_type=jnp.float32)


def kernel(
    sizes,
    dens_ref, mask_ref, start_ref, nodes_ref, forces_ref, weights_ref, stiff_ref,
    pick_ref, spread_ref, keep_ref, pick3_ref, spread3_ref, keep3_ref,
    disp_ref, sens_ref,
    u_f, d_f, q_f, r_f, g_f, u_h, d_h, q_h, r_h, stage,
    terms, before, loads, free, dens_own, dens_side, s_own, s_shift, s_edge,
    m_hi, m_lo, n_hi, n_lo, sums, sums_out, energy, energy_in,
    send_sem, recv_sem, dsend_sem, drecv_sem, psend_sem, precv_sem, esend_sem, erecv_sem,
):
    bricks, cases, count, nx, total_y = sizes
    lanes = count * LANES
    brick = lax.axis_index("brick")
    sub = lax.axis_index("sub")
    case = lax.axis_index("case")
    group = 2 * bricks
    me = 2 * brick + sub
    last = bricks - 1
    other = 1 - sub

    def peer(k):
        target = lax.rem(me + k, group)
        return {"brick": target // 2, "sub": lax.rem(target, 2)}

    def case_peer(k):
        return {"case": lax.rem(case + k, cases)}

    barrier = pltpu.get_barrier_semaphore()
    for k in range(1, group):
        pl.semaphore_signal(barrier, inc=1, device_id=peer(k), device_id_type=MESH)
    for k in range(1, cases):
        pl.semaphore_signal(barrier, inc=1, device_id=case_peer(k), device_id_type=MESH)

    def remote(src, dst, send, recv, device):
        return pltpu.make_async_remote_copy(
            src_ref=src, dst_ref=dst, send_sem=send, recv_sem=recv,
            device_id=device, device_id_type=MESH,
        )

    lower = {"brick": brick - 1}
    upper = {"brick": brick + 1}
    lower_side = {"brick": brick - 1, "sub": other}
    upper_side = {"brick": brick + 1, "sub": other}

    def halo_copies(k, field, rows):
        def sems(n):
            return send_sem.at[k, n], recv_sem.at[k, n]

        return (
            remote(stage.at[k], rows.at[pl.ds(1, nx)], *sems(0), {"sub": other}),
            remote(field.at[1], field.at[nx + 1], *sems(1), lower),
            remote(stage.at[k, 0], rows.at[nx + 1], *sems(2), lower_side),
            remote(field.at[nx], field.at[0], *sems(3), upper),
            remote(stage.at[k, nx - 1], rows.at[0], *sems(4), upper_side),
        )

    def send_halo(k, field, rows):
        line = 7 * (1 - sub)
        stage[k] = jnp.zeros((nx, ROWS, lanes), jnp.float32)
        for x in range(nx):
            for comp in range(3):
                stage[k, x, comp : comp + 1, :] = field[x + 1, pl.ds(8 * comp + line, 1), :]
        copies = halo_copies(k, field, rows)
        copies[0].start()

        @pl.when(brick > 0)
        def _():
            copies[1].start()
            copies[2].start()

        @pl.when(brick < last)
        def _():
            copies[3].start()
            copies[4].start()

    def wait_halo(k, field, rows):
        copies = halo_copies(k, field, rows)
        copies[0].wait()

        @pl.when(brick > 0)
        def _():
            copies[1].wait_send()
            copies[2].wait_send()
            copies[3].wait_recv()
            copies[4].wait_recv()

        @pl.when(brick < last)
        def _():
            copies[3].wait_send()
            copies[4].wait_send()
            copies[1].wait_recv()
            copies[2].wait_recv()

    def density_copies():
        return (
            remote(dens_ref, dens_side.at[pl.ds(1, nx)], dsend_sem.at[0], drecv_sem.at[0], {"sub": other}),
            remote(dens_ref.at[nx - 1], dens_own.at[0], dsend_sem.at[1], drecv_sem.at[1], upper),
            remote(dens_ref.at[nx - 1], dens_side.at[0], dsend_sem.at[2], drecv_sem.at[2], upper_side),
        )

    def sum_copies(k):
        return [
            remote(sums_out.at[k], sums.at[k, n - 1], psend_sem.at[k, n - 1], precv_sem.at[k, n - 1], peer(n))
            for n in range(1, group)
        ]

    def send_sums(k, parts):
        sums_out[k] = jnp.zeros(sums_out.shape[1:], jnp.float32)
        for q, part in enumerate(parts):
            line = jnp.sum(part, axis=0, keepdims=True)
            for c in range(count):
                row = q * count + c
                sums_out[k, row : row + 1, :] = line[:, c * LANES : (c + 1) * LANES]
        for copy in sum_copies(k):
            copy.start()

    def wait_sums(k):
        for copy in sum_copies(k):
            copy.wait()
        total = sums_out[k]
        for n in range(group - 1):
            total = total + sums[k, n]
        return jnp.sum(total, axis=1, keepdims=True)

    def widen(column):
        return jnp.concatenate(
            [jnp.broadcast_to(column[c : c + 1], (1, LANES)) for c in range(count)], axis=1
        )

    def over_cases(tile):
        return jnp.concatenate([tile] * count, axis=1)

    for x in range(nx):
        for comp in range(3):
            tile = (1 - mask_ref[comp, x]).astype(jnp.float32)
            free[x, 8 * comp : 8 * comp + 8, :] = tile
            for c in range(count):
                u_f[x + 1, 8 * comp : 8 * comp + 8, c * LANES : (c + 1) * LANES] = (
                    start_ref[c, comp, x] * tile
                )
    no_plane = jnp.zeros((24, lanes), jnp.float32)
    no_rows = jnp.zeros((ROWS, lanes), jnp.float32)
    no_tile = jnp.zeros((ROWS, LANES), jnp.float32)

    @pl.when(brick == 0)
    def _():
        for field in (u_f, d_f, q_f):
            field[0] = no_plane
        for rows in (u_h, d_h, q_h):
            rows[0] = no_rows
        dens_own[0] = no_tile
        dens_side[0] = no_tile

    @pl.when(brick == last)
    def _():
        for field in (u_f, d_f, q_f):
            field[nx + 1] = no_plane
        for rows in (u_h, d_h, q_h):
            rows[nx + 1] = no_rows

    pl.semaphore_wait(barrier, group - 1 + cases - 1)
    send_halo(0, u_f, u_h)
    copies = density_copies()
    copies[0].start()

    @pl.when(brick < last)
    def _():
        copies[1].start()
        copies[2].start()

    stiff = stiff_ref[...]
    spread_stiff = exact_dot(stiff, spread_ref[sub])
    matrix = keep_ref[sub, 0] * exact_dot(pick_ref[0], spread_stiff)
    matrix = matrix + keep_ref[sub, 1] * exact_dot(pick_ref[1], spread_stiff)
    m_hi[...], m_lo[...] = split(matrix)
    matrix = None
    for b in (0, 1):
        part = keep3_ref[sub, b] * exact_dot(pick3_ref[...], exact_dot(stiff, spread3_ref[b]))
        matrix = part if matrix is None else matrix + part
    high, low = split(matrix)
    n_hi[...] = high
    n_lo[...] = low

    y_bits = int(total_y).bit_length() - 1
    z_bits = LANES.bit_length() - 1
    load_count = nodes_ref.shape[1]
    for c in range(count):
        node = nodes_ref[c : c + 1, :]
        place_z = node & (LANES - 1)
        place_y = ((node >> z_bits) & (total_y - 1)) - sub * ROWS
        place_x = (node >> (z_bits + y_bits)) - brick * nx
        inside = (place_y >= 0) & (place_y < ROWS) & (place_x >= 0) & (place_x < nx)
        place = jnp.where(inside, place_x * ROWS + place_y, -1)
        hit = lax.broadcasted_iota(jnp.int32, (nx * ROWS, load_count), 0) == place
        depth = lax.broadcasted_iota(jnp.int32, (LANES, load_count), 0) == place_z
        depth = jnp.where(depth, 1.0, 0.0).astype(jnp.bfloat16)
        for comp in range(3):
            force = forces_ref[c, comp : comp + 1, :].astype(jnp.float32)
            weighted = jnp.where(hit, force, 0.0).astype(jnp.bfloat16)
            block = lax.dot_general(
                weighted, depth, (((1,), (1,)), ((), ())), preferred_element_type=jnp.float32
            )
            for x in range(nx):
                loads[x, 8 * comp : 8 * comp + 8, c * LANES : (c + 1) * LANES] = block[8 * x : 8 * x + 8]

    copies = density_copies()
    copies[0].wait()

    @pl.when(brick < last)
    def _():
        copies[1].wait_send()
        copies[2].wait_send()

    @pl.when(brick > 0)
    def _():
        copies[1].wait_recv()
        copies[2].wait_recv()

    row_number = lax.broadcasted_iota(jnp.int32, (ROWS, LANES), 0)
    dens_own[1 : nx + 1] = dens_ref[...]
    for i in range(nx + 1):
        def scale_of(density):
            scale = SOFT_FLOOR + (1.0 - SOFT_FLOOR) * (density * density * density)
            return jnp.where(brick > 0, scale, 0.0) if i == 0 else scale

        own = scale_of(dens_own[i])
        below = jnp.where(sub > 0, scale_of(dens_side[i]), 0.0)
        own_edge = jnp.broadcast_to(own[7:8], (ROWS, LANES))
        below_edge = jnp.broadcast_to(below[7:8], (ROWS, LANES))
        s_own[i] = own
        s_shift[i] = jnp.where(row_number == 0, below_edge, pltpu.roll(own, 1, 0))
        s_edge[i] = jnp.where(sub > 0, below_edge, own_edge)

    def by_case(value, shift, edge):
        parts = []
        for c in range(count):
            part = value[:, c * LANES : (c + 1) * LANES]
            part = pltpu.roll(part, shift, 1)
            at = lax.broadcasted_iota(jnp.int32, part.shape, 1)
            parts.append(jnp.where(at == edge, 0.0, part))
        return jnp.concatenate(parts, axis=1)

    def ahead(value):
        return by_case(value, LANES - 1, LANES - 1)

    def behind(value):
        return by_case(value, 1, 0)

    def prepare(p, field, rows):
        value = field[p]
        edge = rows[p]
        terms[p, 0:24, :] = value
        terms[p, 24:48, :] = ahead(value)
        terms[p, 48:56, :] = edge
        terms[p, 56:64, :] = ahead(edge)

    def layer_forces(i):
        own = over_cases(s_own[i])[None]
        shift = over_cases(s_shift[i])[None]
        edge = over_cases(s_edge[i])[None]
        parts = []
        for a in (0, 1):
            main = terms[i + a, 0:48, :].reshape(6, ROWS, lanes)
            side = terms[i + a, 48:64, :].reshape(2, ROWS, lanes)
            parts += [main * own, main * shift, side * edge]
        high, low = split(jnp.concatenate(parts, axis=0).reshape(224, lanes))
        return dot16(m_hi[...], high) + dot16(m_hi[...], low) + dot16(m_lo[...], high)

    def element_pass(field, rows, take, init):
        prepare(0, field, rows)
        prepare(1, field, rows)
        before[...] = layer_forces(0)[48:96]

        def step(i, carry):
            prepare(i + 1, field, rows)
            out = layer_forces(i)
            total = out[0:48] + before[...]
            before[...] = out[48:96]
            return take(i, total[0:24] + behind(total[24:48]), carry)

        return lax.fori_loop(1, nx + 1, step, init)

    def fold(value):
        return value[0:8] + value[8:16] + value[16:24]

    wait_halo(0, u_f, u_h)

    def take_start(i, force, carry):
        residual = (loads[i - 1] - force) * over_cases(free[i - 1])
        d_f[i] = residual
        return carry + fold(residual * residual)

    norm_part = element_pass(u_f, u_h, take_start, no_rows)
    send_halo(1, d_f, d_h)
    wait_halo(1, d_f, d_h)

    def take_first(i, force, carry):
        image = force * over_cases(free[i - 1])
        q_f[i] = image
        return carry + fold(image * d_f[i])

    inner_part = element_pass(d_f, d_h, take_first, no_rows)
    send_sums(0, (inner_part, norm_part))
    send_halo(2, q_f, q_h)
    total = wait_sums(0)
    norm_now = total[count : 2 * count]
    step_length = widen(norm_now / total[0:count])
    norm_part = no_rows
    for x in range(1, nx + 1):
        residual = d_f[x] - step_length * q_f[x]
        r_f[x] = residual
        norm_part = norm_part + fold(residual * residual)
    send_sums(1, (norm_part,))
    wait_halo(2, q_f, q_h)
    for x in (0, nx + 1):
        r_f[x] = d_f[x] - step_length * q_f[x]
    for x in range(nx + 2):
        r_h[x] = d_h[x] - step_length * q_h[x]
        u_f[x] = u_f[x] + step_length * d_f[x]
        u_h[x] = u_h[x] + step_length * d_h[x]

    def take_second(i, force, carry):
        g_f[i - 1] = force * over_cases(free[i - 1])
        return carry

    element_pass(r_f, r_h, take_second, 0)
    norm_next = wait_sums(1)[0:count]
    ratio = widen(norm_next / norm_now)
    inner_part = no_rows
    for x in range(1, nx + 1):
        direction = r_f[x] + ratio * d_f[x]
        r_f[x] = direction
        inner_part = inner_part + fold(direction * (g_f[x - 1] + ratio * q_f[x]))
    send_sums(2, (inner_part,))
    for x in (0, nx + 1):
        r_f[x] = r_f[x] + ratio * d_f[x]
    for x in range(nx + 2):
        r_h[x] = r_h[x] + ratio * d_h[x]
    step_length = widen(norm_next / wait_sums(2)[0:count])
    for x in range(nx + 2):
        moved = u_f[x] + step_length * r_f[x]
        u_f[x] = moved
        u_h[x] = u_h[x] + step_length * r_h[x]
        if 1 <= x <= nx:
            for c in range(count):
                for comp in range(3):
                    disp_ref[c, comp, x - 1] = moved[
                        8 * comp : 8 * comp + 8, c * LANES : (c + 1) * LANES
                    ]

    weights = [weights_ref[case * count + c].astype(jnp.float32) for c in range(count)]
    wide_rows = lax.broadcasted_iota(jnp.int32, (ROWS, lanes), 0)

    def raised(p):
        edge_on = jnp.where(sub == 0, 1.0, 0.0)
        blocks = []
        for c in (0, 1):
            edge = terms[p, 48 + 8 * c : 56 + 8 * c, :] * edge_on
            for comp in range(3):
                start = 24 * c + 8 * comp
                block = pltpu.roll(terms[p, start : start + 8, :], 7, 0)
                blocks.append(jnp.where(wide_rows == 7, edge[comp : comp + 1], block))
        return jnp.concatenate(blocks, axis=0)

    prepare(1, u_f, u_h)

    def energy_step(i, carry):
        prepare(i + 1, u_f, u_h)
        both = terms[pl.ds(i, 2)].reshape(128, lanes)
        high, low = split(both)
        out = dot16(n_hi[...], high) + dot16(n_hi[...], low) + dot16(n_lo[...], high)
        found = no_rows
        for a in (0, 1):
            for b in (0, 1):
                value = raised(i + a) if b else terms[i + a, 0:48, :]
                base = 96 * a + 48 * b
                product = (value * out[base : base + 48]).reshape(6, ROWS, lanes)
                found = found + jnp.sum(product, axis=0)
        weighted = no_tile
        for c in range(count):
            weighted = weighted + weights[c] * found[:, c * LANES : (c + 1) * LANES]
        energy[i - 1] = weighted
        return carry

    lax.fori_loop(1, nx + 1, energy_step, 0)

    copies = [
        remote(energy, energy_in.at[n - 1], esend_sem.at[n - 1], erecv_sem.at[n - 1], case_peer(n))
        for n in range(1, cases)
    ]
    for copy in copies:
        copy.start()
    for copy in copies:
        copy.wait()
    weight_sum = weights_ref[0].astype(jnp.float32)
    for n in range(1, weights_ref.shape[0]):
        weight_sum = weight_sum + weights_ref[n].astype(jnp.float32)
    share = LANES // cases
    for x in range(nx):
        total = energy[x]
        for n in range(cases - 1):
            total = total + energy_in[n, x]
        density = dens_ref[x]
        result = -(PENALTY * (1.0 - SOFT_FLOOR)) * (density * density) * total / weight_sum
        owned = result[:, 0:share]
        for n in range(1, cases):
            owned = jnp.where(case == n, result[:, n * share : (n + 1) * share], owned)
        sens_ref[x] = owned


def per_device(
    mesh_shape, densities, fixed_mask, start_field, load_nodes, load_forces, case_weights, stiffness
):
    bricks, cases = mesh_shape["brick"], mesh_shape["case"]
    assert mesh_shape["sub"] == 2
    count, _, nx, ny, nz = start_field.shape
    assert ny == ROWS and nz == LANES
    lanes = count * LANES
    group = 2 * bricks
    sum_rows = -(-2 * count // 8) * 8
    pick, spread, keep = force_constants()
    pick3, spread3, keep3 = energy_constants()
    f32, bf16 = jnp.float32, jnp.bfloat16
    vmem = pl.BlockSpec(memory_space=pltpu.VMEM)
    smem = pl.BlockSpec(memory_space=pltpu.SMEM)
    dma = pltpu.SemaphoreType.DMA
    plane = pltpu.VMEM((nx + 2, 24, lanes), f32)
    rows = pltpu.VMEM((nx + 2, ROWS, lanes), f32)
    scales = pltpu.VMEM((nx + 1, ROWS, LANES), f32)
    return pl.pallas_call(
        functools.partial(kernel, (bricks, cases, count, nx, 2 * ROWS)),
        out_shape=(
            jax.ShapeDtypeStruct(start_field.shape, f32),
            jax.ShapeDtypeStruct((nx, ROWS, LANES // cases), f32),
        ),
        in_specs=[vmem] * 5 + [smem] + [vmem] * 7,
        out_specs=(vmem, vmem),
        scratch_shapes=[
            plane, plane, plane, plane,
            pltpu.VMEM((nx, 24, lanes), f32),
            rows, rows, rows, rows,
            pltpu.VMEM((3, nx, ROWS, lanes), f32),
            pltpu.VMEM((nx + 2, 64, lanes), f32),
            pltpu.VMEM((48, lanes), f32),
            pltpu.VMEM((nx, 24, lanes), f32),
            pltpu.VMEM((nx, 24, LANES), f32),
            scales, scales, scales, scales, scales,
            pltpu.VMEM((96, 224), bf16),
            pltpu.VMEM((96, 224), bf16),
            pltpu.VMEM((192, 128), bf16),
            pltpu.VMEM((192, 128), bf16),
            pltpu.VMEM((3, group - 1, sum_rows, LANES), f32),
            pltpu.VMEM((3, sum_rows, LANES), f32),
            pltpu.VMEM((nx, ROWS, LANES), f32),
            pltpu.VMEM((max(cases - 1, 1), nx, ROWS, LANES), f32),
            dma((3, 5)), dma((3, 5)), dma((3,)), dma((3,)),
            dma((3, group - 1)), dma((3, group - 1)),
            dma((max(cases - 1, 1),)), dma((max(cases - 1, 1),)),
        ],
        compiler_params=pltpu.CompilerParams(
            collective_id=0, has_side_effects=True, vmem_limit_bytes=40 * 2**20
        ),
    )(
        densities, fixed_mask, start_field, load_nodes, jnp.swapaxes(load_forces, 1, 2),
        case_weights, stiffness, *(jnp.asarray(x) for x in (pick, spread, keep, pick3, spread3, keep3)),
    )


def solution(mesh):
    return jax.shard_map(
        functools.partial(per_device, dict(mesh.shape)),
        mesh=mesh,
        in_specs=(
            P(("design", "brick"), "sub", None),
            P(None, ("design", "brick"), "sub", None),
            P("case", None, ("design", "brick"), "sub", None),
            P("case", None),
            P("case", None, None),
            P(),
            P(),
        ),
        out_specs=(
            P("case", None, ("design", "brick"), "sub", None),
            P(("design", "brick"), "sub", "case"),
        ),
        check_vma=False,
    )
```

```python
import functools

import jax
import jax.numpy as jnp
import numpy as np
from jax import lax
from jax.experimental import pallas as pl
from jax.experimental.pallas import tpu as pltpu
from jax.sharding import PartitionSpec as P

PENALTY = 3.0
SOFT_FLOOR = 0.001
MESH = pl.DeviceIdType.MESH
UNROLL = 6
ENERGY_UNROLL = 8
VMEM_BYTES = 63 * 2**20 + 2**19
ROWS = 8
LANES = 128


def corner_index(a, b, c, comp):
    return 3 * (4 * a + 2 * b + c) + comp


def force_constants():
    pick = np.zeros((2, 96, 24), np.float32)
    spread = np.zeros((2, 24, 224), np.float32)
    keep = np.zeros((2, 2, 96, 224), np.float32)
    rows = []
    for a in (0, 1):
        for c in (0, 1):
            for comp in range(3):
                for y in range(ROWS):
                    for b in (0, 1):
                        pick[b, len(rows), corner_index(a, b, c, comp)] = 1
                    rows.append(y)
    for side in (0, 1):
        columns = []
        for a in (0, 1):
            for b in (0, 1):
                for c in (0, 1):
                    for comp in range(3):
                        for y in range(ROWS):
                            columns.append((corner_index(a, b, c, comp), y - b))
            for c in (0, 1):
                for comp in range(ROWS):
                    if comp < 3:
                        b = 1 - side
                        columns.append((corner_index(a, b, c, comp), 7 if side == 0 else -1))
                    else:
                        columns.append(None)
        for n, column in enumerate(columns):
            if column is None:
                continue
            spread[side, column[0], n] = 1
            for m, y in enumerate(rows):
                if y - column[1] in (0, 1):
                    keep[side, y - column[1], m, n] = 1
    return pick, spread, keep


def energy_constants():
    pick = np.zeros((192, 24), np.float32)
    spread = np.zeros((2, 24, 128), np.float32)
    keep = np.zeros((2, 2, 192, 128), np.float32)
    for j in range(24):
        pick[8 * j : 8 * j + 8, j] = 1
    for side in (0, 1):
        for a in (0, 1):
            for c in (0, 1):
                for comp in range(3):
                    for b in (0, 1):
                        for y in range(ROWS):
                            n = 64 * a + 24 * c + 8 * comp + y
                            spread[b, corner_index(a, b, c, comp), n] = 1
                            if y - b >= 0:
                                keep[side, b, y - b :: 8, n] = 1
                        n = 64 * a + 48 + 8 * c + comp
                        spread[b, corner_index(a, b, c, comp), n] = 1
                        if side == 0 and b == 1:
                            keep[side, b, 7::8, n] = 1
    return pick, spread, keep


def split(value):
    high = value.astype(jnp.bfloat16)
    return high, (value - high.astype(jnp.float32)).astype(jnp.bfloat16)


def exact_dot(a, b):
    return jnp.dot(a, b, precision=lax.Precision.HIGHEST, preferred_element_type=jnp.float32)


def dot16(a, b):
    return jnp.dot(a, b, preferred_element_type=jnp.float32)


def kernel(
    sizes,
    dens_hbm, mask_hbm, start_hbm, nodes_hbm, forces_hbm, weights_hbm, stiff_hbm,
    pick_hbm, spread_hbm, keep_hbm, pick3_hbm, spread3_hbm, keep3_hbm,
    disp_ref, sens_ref,
    dens_ref, mask_ref, start_ref, nodes_ref, forces_ref, weights_ref, stiff_ref,
    pick_ref, spread_ref, keep_ref, pick3_ref, spread3_ref, keep3_ref, load_sem, first,
    u_f, d_f, q_f, r_f, g_f, u_h, d_h, q_h, r_h, stage,
    terms, before, loads, free, dens_own, dens_side, s_own, s_shift, s_edge,
    m_hi, m_lo, n_hi, n_lo, sums, sums_out, energy, energy_in,
    send_sem, recv_sem, dsend_sem, drecv_sem, psend_sem, precv_sem, esend_sem, erecv_sem,
):
    bricks, cases, count, nx, total_y = sizes
    lanes = count * LANES
    brick = lax.axis_index("brick")
    sub = lax.axis_index("sub")
    case = lax.axis_index("case")
    group = 2 * bricks
    me = 2 * brick + sub
    last = bricks - 1
    other = 1 - sub

    def peer(k):
        target = lax.rem(me + k, group)
        return {"brick": target // 2, "sub": lax.rem(target, 2)}

    def case_peer(k):
        return {"case": lax.rem(case + k, cases)}

    inputs = (
        (start_hbm, start_ref), (mask_hbm, mask_ref), (dens_hbm, dens_ref),
        (stiff_hbm, stiff_ref), (spread_hbm.at[sub], spread_ref), (pick_hbm, pick_ref),
        (keep_hbm.at[sub], keep_ref), (spread3_hbm, spread3_ref), (pick3_hbm, pick3_ref),
        (keep3_hbm.at[sub], keep3_ref), (nodes_hbm, nodes_ref), (forces_hbm, forces_ref),
        (weights_hbm, weights_ref),
    )
    fetches = [
        pltpu.make_async_copy(src, dst, load_sem.at[n]) for n, (src, dst) in enumerate(inputs)
    ]
    for fetch in fetches:
        fetch.start()

    barrier = pltpu.get_barrier_semaphore()
    for k in range(1, group):
        pl.semaphore_signal(barrier, inc=1, device_id=peer(k), device_id_type=MESH)
    for k in range(1, cases):
        pl.semaphore_signal(barrier, inc=1, device_id=case_peer(k), device_id_type=MESH)

    def remote(src, dst, send, recv, device):
        return pltpu.make_async_remote_copy(
            src_ref=src, dst_ref=dst, send_sem=send, recv_sem=recv,
            device_id=device, device_id_type=MESH,
        )

    lower = {"brick": brick - 1}
    upper = {"brick": brick + 1}
    lower_side = {"brick": brick - 1, "sub": other}
    upper_side = {"brick": brick + 1, "sub": other}

    def halo_copies(k, field, rows):
        def sems(n):
            return send_sem.at[k, n], recv_sem.at[k, n]

        return (
            remote(stage.at[k], rows.at[pl.ds(1, nx)], *sems(0), {"sub": other}),
            remote(field.at[1], field.at[nx + 1], *sems(1), lower),
            remote(stage.at[k, 0], rows.at[nx + 1], *sems(2), lower_side),
            remote(field.at[nx], field.at[0], *sems(3), upper),
            remote(stage.at[k, nx - 1], rows.at[0], *sems(4), upper_side),
        )

    def send_halo(k, field, rows):
        line = 7 * (1 - sub)
        stage[k] = jnp.zeros((nx, ROWS, lanes), jnp.float32)
        for x in range(nx):
            for comp in range(3):
                stage[k, x, comp : comp + 1, :] = field[x + 1, pl.ds(8 * comp + line, 1), :]
        copies = halo_copies(k, field, rows)
        copies[0].start()

        @pl.when(brick > 0)
        def _():
            copies[1].start()
            copies[2].start()

        @pl.when(brick < last)
        def _():
            copies[3].start()
            copies[4].start()

    def wait_side(k, field, rows):
        halo_copies(k, field, rows)[0].wait()

    def wait_ends(k, field, rows):
        copies = halo_copies(k, field, rows)

        @pl.when(brick > 0)
        def _():
            copies[1].wait_send()
            copies[2].wait_send()
            copies[3].wait_recv()
            copies[4].wait_recv()

        @pl.when(brick < last)
        def _():
            copies[3].wait_send()
            copies[4].wait_send()
            copies[1].wait_recv()
            copies[2].wait_recv()

    def density_copies():
        return (
            remote(dens_ref, dens_side.at[pl.ds(1, nx)], dsend_sem.at[0], drecv_sem.at[0], {"sub": other}),
            remote(dens_ref.at[nx - 1], dens_own.at[0], dsend_sem.at[1], drecv_sem.at[1], upper),
            remote(dens_ref.at[nx - 1], dens_side.at[0], dsend_sem.at[2], drecv_sem.at[2], upper_side),
        )

    def sum_copies(k):
        return [
            remote(sums_out.at[k], sums.at[k, n - 1], psend_sem.at[k, n - 1], precv_sem.at[k, n - 1], peer(n))
            for n in range(1, group)
        ]

    def send_sums(k, parts):
        sums_out[k] = jnp.zeros(sums_out.shape[1:], jnp.float32)
        for q, part in enumerate(parts):
            line = jnp.sum(part, axis=0, keepdims=True)
            for c in range(count):
                row = q * count + c
                sums_out[k, row : row + 1, :] = line[:, c * LANES : (c + 1) * LANES]
        for copy in sum_copies(k):
            copy.start()

    def wait_sums(k):
        for copy in sum_copies(k):
            copy.wait()
        total = sums_out[k]
        for n in range(group - 1):
            total = total + sums[k, n]
        return jnp.sum(total, axis=1, keepdims=True)

    def widen(column):
        return jnp.concatenate(
            [jnp.broadcast_to(column[c : c + 1], (1, LANES)) for c in range(count)], axis=1
        )

    def over_cases(tile):
        return jnp.concatenate([tile] * count, axis=1)

    fetches[0].wait()
    fetches[1].wait()

    for x in range(nx):
        for comp in range(3):
            tile = (1 - mask_ref[comp, x]).astype(jnp.float32)
            free[x, 8 * comp : 8 * comp + 8, :] = tile
            for c in range(count):
                u_f[x + 1, 8 * comp : 8 * comp + 8, c * LANES : (c + 1) * LANES] = (
                    start_ref[c, comp, x] * tile
                )
    no_plane = jnp.zeros((24, lanes), jnp.float32)
    no_rows = jnp.zeros((ROWS, lanes), jnp.float32)
    no_tile = jnp.zeros((ROWS, LANES), jnp.float32)

    @pl.when(brick == 0)
    def _():
        for field in (u_f, d_f, q_f):
            field[0] = no_plane
        for rows in (u_h, d_h, q_h):
            rows[0] = no_rows
        dens_own[0] = no_tile
        dens_side[0] = no_tile

    @pl.when(brick == last)
    def _():
        for field in (u_f, d_f, q_f):
            field[nx + 1] = no_plane
        for rows in (u_h, d_h, q_h):
            rows[nx + 1] = no_rows

    pl.semaphore_wait(barrier, group - 1 + cases - 1)
    send_halo(0, u_f, u_h)
    fetches[2].wait()
    copies = density_copies()
    copies[0].start()

    @pl.when(brick < last)
    def _():
        copies[1].start()
        copies[2].start()

    for fetch in fetches[3:]:
        fetch.wait()
    stiff = stiff_ref[...]
    spread_stiff = exact_dot(stiff, spread_ref[...])
    matrix = keep_ref[0] * exact_dot(pick_ref[0], spread_stiff)
    matrix = matrix + keep_ref[1] * exact_dot(pick_ref[1], spread_stiff)
    m_hi[...], m_lo[...] = split(matrix)
    matrix = None
    for b in (0, 1):
        part = keep3_ref[b] * exact_dot(pick3_ref[...], exact_dot(stiff, spread3_ref[b]))
        matrix = part if matrix is None else matrix + part
    high, low = split(matrix)
    n_hi[...] = high
    n_lo[...] = low

    y_bits = int(total_y).bit_length() - 1
    z_bits = LANES.bit_length() - 1
    load_count = nodes_ref.shape[1]
    for c in range(count):
        node = nodes_ref[c : c + 1, :]
        place_z = node & (LANES - 1)
        place_y = ((node >> z_bits) & (total_y - 1)) - sub * ROWS
        place_x = (node >> (z_bits + y_bits)) - brick * nx
        inside = (place_y >= 0) & (place_y < ROWS) & (place_x >= 0) & (place_x < nx)
        place = jnp.where(inside, place_x * ROWS + place_y, -1)
        hit = lax.broadcasted_iota(jnp.int32, (nx * ROWS, load_count), 0) == place
        depth = lax.broadcasted_iota(jnp.int32, (LANES, load_count), 0) == place_z
        depth = jnp.where(depth, 1.0, 0.0).astype(jnp.bfloat16)
        for comp in range(3):
            force = forces_ref[comp, c : c + 1, :].astype(jnp.float32)
            weighted = jnp.where(hit, force, 0.0).astype(jnp.bfloat16)
            block = lax.dot_general(
                weighted, depth, (((1,), (1,)), ((), ())), preferred_element_type=jnp.float32
            )
            for x in range(nx):
                loads[x, 8 * comp : 8 * comp + 8, c * LANES : (c + 1) * LANES] = block[8 * x : 8 * x + 8]

    density_copies()[0].wait()
    row_number = lax.broadcasted_iota(jnp.int32, (ROWS, LANES), 0)
    dens_own[1 : nx + 1] = dens_ref[...]

    def layer_scale(i):
        def scale_of(density):
            scale = SOFT_FLOOR + (1.0 - SOFT_FLOOR) * (density * density * density)
            return jnp.where(brick > 0, scale, 0.0) if i == 0 else scale

        own = scale_of(dens_own[i])
        below = jnp.where(sub > 0, scale_of(dens_side[i]), 0.0)
        own_edge = jnp.broadcast_to(own[7:8], (ROWS, LANES))
        below_edge = jnp.broadcast_to(below[7:8], (ROWS, LANES))
        s_own[i] = own
        s_shift[i] = jnp.where(row_number == 0, below_edge, pltpu.roll(own, 1, 0))
        s_edge[i] = jnp.where(sub > 0, below_edge, own_edge)

    for i in range(1, nx + 1):
        layer_scale(i)

    def by_case(value, shift, edge):
        parts = []
        for c in range(count):
            part = value[:, c * LANES : (c + 1) * LANES]
            part = pltpu.roll(part, shift, 1)
            at = lax.broadcasted_iota(jnp.int32, part.shape, 1)
            parts.append(jnp.where(at == edge, 0.0, part))
        return jnp.concatenate(parts, axis=1)

    def ahead(value):
        return by_case(value, LANES - 1, LANES - 1)

    def behind(value):
        return by_case(value, 1, 0)

    def prepare(p, field, rows):
        value = field[p]
        edge = rows[p]
        terms[p, 0:24, :] = value
        terms[p, 24:48, :] = ahead(value)
        terms[p, 48:56, :] = edge
        terms[p, 56:64, :] = ahead(edge)

    def layer_forces(i):
        own = over_cases(s_own[i])[None]
        shift = over_cases(s_shift[i])[None]
        edge = over_cases(s_edge[i])[None]
        parts = []
        for a in (0, 1):
            main = terms[i + a, 0:48, :].reshape(6, ROWS, lanes)
            side = terms[i + a, 48:64, :].reshape(2, ROWS, lanes)
            parts += [main * own, main * shift, side * edge]
        high, low = split(jnp.concatenate(parts, axis=0).reshape(224, lanes))
        return dot16(m_hi[...], high) + dot16(m_hi[...], low) + dot16(m_lo[...], high)

    def element_pass(field, rows, ends, take, init):
        prepare(1, field, rows)
        prepare(2, field, rows)
        out = layer_forces(1)
        first[...] = out[0:48]
        before[...] = out[48:96]

        def step(i, carry):
            out = layer_forces(i)
            total = out[0:48] + before[...]
            before[...] = out[48:96]
            return take(i, total[0:24] + behind(total[24:48]), carry)

        def inner(i, carry):
            prepare(i + 1, field, rows)
            return step(i, carry)

        carry = lax.fori_loop(2, nx, inner, init, unroll=UNROLL)
        ends()
        prepare(0, field, rows)
        prepare(nx + 1, field, rows)
        total = first[...] + layer_forces(0)[48:96]
        carry = take(1, total[0:24] + behind(total[24:48]), carry)
        return step(nx, carry)

    def fold(value):
        return value[0:8] + value[8:16] + value[16:24]

    wait_side(0, u_f, u_h)

    def start_ends():
        copies = density_copies()

        @pl.when(brick < last)
        def _():
            copies[1].wait_send()
            copies[2].wait_send()

        @pl.when(brick > 0)
        def _():
            copies[1].wait_recv()
            copies[2].wait_recv()

        layer_scale(0)
        wait_ends(0, u_f, u_h)

    def take_start(i, force, carry):
        residual = (loads[i - 1] - force) * over_cases(free[i - 1])
        d_f[i] = residual
        return carry + fold(residual * residual)

    norm_part = element_pass(u_f, u_h, start_ends, take_start, no_rows)
    send_halo(1, d_f, d_h)
    wait_side(1, d_f, d_h)

    def take_first(i, force, carry):
        image = force * over_cases(free[i - 1])
        q_f[i] = image
        return carry + fold(image * d_f[i])

    inner_part = element_pass(d_f, d_h, lambda: wait_ends(1, d_f, d_h), take_first, no_rows)
    send_sums(0, (inner_part, norm_part))
    send_halo(2, q_f, q_h)
    total = wait_sums(0)
    norm_now = total[count : 2 * count]
    step_length = widen(norm_now / total[0:count])
    norm_part = no_rows
    for x in range(1, nx + 1):
        residual = d_f[x] - step_length * q_f[x]
        r_f[x] = residual
        norm_part = norm_part + fold(residual * residual)
    send_sums(1, (norm_part,))
    wait_side(2, q_f, q_h)
    for x in range(1, nx + 1):
        r_h[x] = d_h[x] - step_length * q_h[x]

    def second_ends():
        wait_ends(2, q_f, q_h)
        for x in (0, nx + 1):
            r_f[x] = d_f[x] - step_length * q_f[x]
            r_h[x] = d_h[x] - step_length * q_h[x]

    def take_second(i, force, carry):
        g_f[i - 1] = force * over_cases(free[i - 1])
        return carry

    element_pass(r_f, r_h, second_ends, take_second, 0)
    norm_next = wait_sums(1)[0:count]
    ratio = widen(norm_next / norm_now)
    inner_part = no_rows
    for x in range(1, nx + 1):
        direction = r_f[x] + ratio * d_f[x]
        r_f[x] = direction
        inner_part = inner_part + fold(direction * (g_f[x - 1] + ratio * q_f[x]))
    send_sums(2, (inner_part,))
    r_f[nx + 1] = r_f[nx + 1] + ratio * d_f[nx + 1]
    for x in range(1, nx + 2):
        u_f[x] = u_f[x] + step_length * d_f[x]
        u_h[x] = u_h[x] + step_length * d_h[x]
        r_h[x] = r_h[x] + ratio * d_h[x]
    step_length = widen(norm_next / wait_sums(2)[0:count])
    for x in range(1, nx + 2):
        moved = u_f[x] + step_length * r_f[x]
        u_f[x] = moved
        u_h[x] = u_h[x] + step_length * r_h[x]
        if x <= nx:
            for c in range(count):
                for comp in range(3):
                    disp_ref[c, comp, x - 1] = moved[
                        8 * comp : 8 * comp + 8, c * LANES : (c + 1) * LANES
                    ]

    weights = [weights_ref[case * count + c].astype(jnp.float32) for c in range(count)]
    wide_rows = lax.broadcasted_iota(jnp.int32, (ROWS, lanes), 0)

    def raised(p):
        edge_on = jnp.where(sub == 0, 1.0, 0.0)
        blocks = []
        for c in (0, 1):
            edge = terms[p, 48 + 8 * c : 56 + 8 * c, :] * edge_on
            for comp in range(3):
                start = 24 * c + 8 * comp
                block = pltpu.roll(terms[p, start : start + 8, :], 7, 0)
                blocks.append(jnp.where(wide_rows == 7, edge[comp : comp + 1], block))
        return jnp.concatenate(blocks, axis=0)

    prepare(1, u_f, u_h)

    def energy_step(i, carry):
        prepare(i + 1, u_f, u_h)
        both = terms[pl.ds(i, 2)].reshape(128, lanes)
        high, low = split(both)
        out = dot16(n_hi[...], high) + dot16(n_hi[...], low) + dot16(n_lo[...], high)
        found = no_rows
        for a in (0, 1):
            for b in (0, 1):
                value = raised(i + a) if b else terms[i + a, 0:48, :]
                base = 96 * a + 48 * b
                product = (value * out[base : base + 48]).reshape(6, ROWS, lanes)
                found = found + jnp.sum(product, axis=0)
        weighted = no_tile
        for c in range(count):
            weighted = weighted + weights[c] * found[:, c * LANES : (c + 1) * LANES]
        energy[i - 1] = weighted
        return carry

    lax.fori_loop(1, nx + 1, energy_step, 0, unroll=ENERGY_UNROLL)

    copies = [
        remote(energy, energy_in.at[n - 1], esend_sem.at[n - 1], erecv_sem.at[n - 1], case_peer(n))
        for n in range(1, cases)
    ]
    for copy in copies:
        copy.start()
    for copy in copies:
        copy.wait()
    weight_sum = weights_ref[0].astype(jnp.float32)
    for n in range(1, weights_ref.shape[0]):
        weight_sum = weight_sum + weights_ref[n].astype(jnp.float32)
    share = LANES // cases
    for x in range(nx):
        total = energy[x]
        for n in range(cases - 1):
            total = total + energy_in[n, x]
        density = dens_ref[x]
        result = -(PENALTY * (1.0 - SOFT_FLOOR)) * (density * density) * total / weight_sum
        owned = result[:, 0:share]
        for n in range(1, cases):
            owned = jnp.where(case == n, result[:, n * share : (n + 1) * share], owned)
        sens_ref[x] = owned


def per_device(
    mesh_shape, densities, fixed_mask, start_field, load_nodes, load_forces, case_weights, stiffness
):
    bricks, cases = mesh_shape["brick"], mesh_shape["case"]
    assert mesh_shape["sub"] == 2
    count, _, nx, ny, nz = start_field.shape
    assert ny == ROWS and nz == LANES
    lanes = count * LANES
    group = 2 * bricks
    sum_rows = -(-2 * count // 8) * 8
    pick, spread, keep = force_constants()
    pick3, spread3, keep3 = energy_constants()
    f32, bf16 = jnp.float32, jnp.bfloat16
    vmem = pl.BlockSpec(memory_space=pltpu.VMEM)
    dma = pltpu.SemaphoreType.DMA
    plane = pltpu.VMEM((nx + 2, 24, lanes), f32)
    rows = pltpu.VMEM((nx + 2, ROWS, lanes), f32)
    scales = pltpu.VMEM((nx + 1, ROWS, LANES), f32)
    arguments = (
        densities, fixed_mask, start_field, load_nodes, jnp.transpose(load_forces, (2, 0, 1)),
        case_weights, stiffness,
    )
    return pl.pallas_call(
        functools.partial(kernel, (bricks, cases, count, nx, 2 * ROWS)),
        out_shape=(
            jax.ShapeDtypeStruct(start_field.shape, f32),
            jax.ShapeDtypeStruct((nx, ROWS, LANES // cases), f32),
        ),
        in_specs=[pl.BlockSpec(memory_space=pltpu.HBM)] * 13,
        out_specs=(vmem, vmem),
        scratch_shapes=[
            *(pltpu.VMEM(x.shape, x.dtype) for x in arguments[:5]),
            pltpu.SMEM(case_weights.shape, case_weights.dtype),
            pltpu.VMEM(stiffness.shape, f32),
            pltpu.VMEM(pick.shape, f32), pltpu.VMEM(spread.shape[1:], f32),
            pltpu.VMEM(keep.shape[1:], f32),
            pltpu.VMEM(pick3.shape, f32), pltpu.VMEM(spread3.shape, f32),
            pltpu.VMEM(keep3.shape[1:], f32),
            dma((13,)), pltpu.VMEM((48, lanes), f32),
            plane, plane, plane, plane,
            pltpu.VMEM((nx, 24, lanes), f32),
            rows, rows, rows, rows,
            pltpu.VMEM((3, nx, ROWS, lanes), f32),
            pltpu.VMEM((nx + 2, 64, lanes), f32),
            pltpu.VMEM((48, lanes), f32),
            pltpu.VMEM((nx, 24, lanes), f32),
            pltpu.VMEM((nx, 24, LANES), f32),
            scales, scales, scales, scales, scales,
            pltpu.VMEM((96, 224), bf16),
            pltpu.VMEM((96, 224), bf16),
            pltpu.VMEM((192, 128), bf16),
            pltpu.VMEM((192, 128), bf16),
            pltpu.VMEM((3, group - 1, sum_rows, LANES), f32),
            pltpu.VMEM((3, sum_rows, LANES), f32),
            pltpu.VMEM((nx, ROWS, LANES), f32),
            pltpu.VMEM((max(cases - 1, 1), nx, ROWS, LANES), f32),
            dma((3, 5)), dma((3, 5)), dma((3,)), dma((3,)),
            dma((3, group - 1)), dma((3, group - 1)),
            dma((max(cases - 1, 1),)), dma((max(cases - 1, 1),)),
        ],
        compiler_params=pltpu.CompilerParams(
            collective_id=0, has_side_effects=True, vmem_limit_bytes=VMEM_BYTES
        ),
    )(*arguments, *(jnp.asarray(x) for x in (pick, spread, keep, pick3, spread3, keep3)))


def solution(mesh):
    return jax.shard_map(
        functools.partial(per_device, dict(mesh.shape)),
        mesh=mesh,
        in_specs=(
            P(("design", "brick"), "sub", None),
            P(None, ("design", "brick"), "sub", None),
            P("case", None, ("design", "brick"), "sub", None),
            P("case", None),
            P("case", None, None),
            P(),
            P(),
        ),
        out_specs=(
            P("case", None, ("design", "brick"), "sub", None),
            P(("design", "brick"), "sub", "case"),
        ),
        check_vma=False,
    )
```

```python
import functools

import jax
import jax.numpy as jnp
import numpy as np
from jax import lax
from jax.experimental import pallas as pl
from jax.experimental.pallas import tpu as pltpu
from jax.sharding import PartitionSpec as P

PENALTY = 3.0
SOFT_FLOOR = 0.001
MESH = pl.DeviceIdType.MESH
UNROLL = 6
ENERGY_UNROLL = 8
VMEM_BYTES = 63 * 2**20 + 2**19
ROWS = 8
LANES = 128


def corner_index(a, b, c, comp):
    return 3 * (4 * a + 2 * b + c) + comp


def force_constants():
    pick = np.zeros((2, 96, 24), np.float32)
    spread = np.zeros((2, 24, 224), np.float32)
    keep = np.zeros((2, 2, 96, 224), np.float32)
    rows = []
    for a in (0, 1):
        for c in (0, 1):
            for comp in range(3):
                for y in range(ROWS):
                    for b in (0, 1):
                        pick[b, len(rows), corner_index(a, b, c, comp)] = 1
                    rows.append(y)
    for side in (0, 1):
        columns = []
        for a in (0, 1):
            for b in (0, 1):
                for c in (0, 1):
                    for comp in range(3):
                        for y in range(ROWS):
                            columns.append((corner_index(a, b, c, comp), y - b))
            for c in (0, 1):
                for comp in range(ROWS):
                    if comp < 3:
                        b = 1 - side
                        columns.append((corner_index(a, b, c, comp), 7 if side == 0 else -1))
                    else:
                        columns.append(None)
        for n, column in enumerate(columns):
            if column is None:
                continue
            spread[side, column[0], n] = 1
            for m, y in enumerate(rows):
                if y - column[1] in (0, 1):
                    keep[side, y - column[1], m, n] = 1
    return pick, spread, keep


def energy_constants():
    pick = np.zeros((192, 24), np.float32)
    spread = np.zeros((2, 24, 128), np.float32)
    keep = np.zeros((2, 2, 192, 128), np.float32)
    for j in range(24):
        pick[8 * j : 8 * j + 8, j] = 1
    for side in (0, 1):
        for a in (0, 1):
            for c in (0, 1):
                for comp in range(3):
                    for b in (0, 1):
                        for y in range(ROWS):
                            n = 64 * a + 24 * c + 8 * comp + y
                            spread[b, corner_index(a, b, c, comp), n] = 1
                            if y - b >= 0:
                                keep[side, b, y - b :: 8, n] = 1
                        n = 64 * a + 48 + 8 * c + comp
                        spread[b, corner_index(a, b, c, comp), n] = 1
                        if side == 0 and b == 1:
                            keep[side, b, 7::8, n] = 1
    return pick, spread, keep


def split(value):
    high = value.astype(jnp.bfloat16)
    return high, (value - high.astype(jnp.float32)).astype(jnp.bfloat16)


def exact_dot(a, b):
    return jnp.dot(a, b, precision=lax.Precision.HIGHEST, preferred_element_type=jnp.float32)


def dot16(a, b):
    return jnp.dot(a, b, preferred_element_type=jnp.float32)


def kernel(
    sizes,
    dens_hbm, mask_hbm, start_hbm, nodes_hbm, forces_hbm, weights_hbm, stiff_hbm,
    pick_hbm, spread_hbm, keep_hbm, pick3_hbm, spread3_hbm, keep3_hbm,
    disp_ref, sens_ref,
    dens_ref, mask_ref, start_ref, nodes_ref, forces_ref, weights_ref, stiff_ref,
    pick_ref, spread_ref, keep_ref, pick3_ref, spread3_ref, keep3_ref, load_sem, first,
    u_f, d_f, q_f, r_f, g_f, u_h, d_h, q_h, r_h, stage,
    terms, before, loads, free, dens_own, dens_side, s_own, s_shift, s_edge,
    m_hi, m_lo, n_hi, n_lo, sums, sums_out, energy, energy_in,
    send_sem, recv_sem, dsend_sem, drecv_sem, psend_sem, precv_sem, esend_sem, erecv_sem,
):
    bricks, cases, count, nx, total_y = sizes
    lanes = count * LANES
    brick = lax.axis_index("brick")
    sub = lax.axis_index("sub")
    case = lax.axis_index("case")
    group = 2 * bricks
    me = 2 * brick + sub
    last = bricks - 1
    other = 1 - sub

    def peer(k):
        target = lax.rem(me + k, group)
        return {"brick": target // 2, "sub": lax.rem(target, 2)}

    def case_peer(k):
        return {"case": lax.rem(case + k, cases)}

    inputs = (
        (start_hbm, start_ref), (mask_hbm, mask_ref), (dens_hbm, dens_ref),
        (stiff_hbm, stiff_ref), (spread_hbm.at[sub], spread_ref), (pick_hbm, pick_ref),
        (keep_hbm.at[sub], keep_ref), (spread3_hbm, spread3_ref), (pick3_hbm, pick3_ref),
        (keep3_hbm.at[sub], keep3_ref), (nodes_hbm, nodes_ref), (forces_hbm, forces_ref),
        (weights_hbm, weights_ref),
    )
    fetches = [
        pltpu.make_async_copy(src, dst, load_sem.at[n]) for n, (src, dst) in enumerate(inputs)
    ]
    for fetch in fetches:
        fetch.start()

    barrier = pltpu.get_barrier_semaphore()
    for k in range(1, group):
        pl.semaphore_signal(barrier, inc=1, device_id=peer(k), device_id_type=MESH)
    for k in range(1, cases):
        pl.semaphore_signal(barrier, inc=1, device_id=case_peer(k), device_id_type=MESH)

    def remote(src, dst, send, recv, device):
        return pltpu.make_async_remote_copy(
            src_ref=src, dst_ref=dst, send_sem=send, recv_sem=recv,
            device_id=device, device_id_type=MESH,
        )

    lower = {"brick": brick - 1}
    upper = {"brick": brick + 1}
    lower_side = {"brick": brick - 1, "sub": other}
    upper_side = {"brick": brick + 1, "sub": other}

    def halo_copies(k, field, rows):
        def sems(n):
            return send_sem.at[k, n], recv_sem.at[k, n]

        return (
            remote(stage.at[k], rows.at[pl.ds(1, nx)], *sems(0), {"sub": other}),
            remote(field.at[1], field.at[nx + 1], *sems(1), lower),
            remote(stage.at[k, 0], rows.at[nx + 1], *sems(2), lower_side),
            remote(field.at[nx], field.at[0], *sems(3), upper),
            remote(stage.at[k, nx - 1], rows.at[0], *sems(4), upper_side),
        )

    def send_halo(k, field, rows):
        line = 7 * (1 - sub)
        stage[k] = jnp.zeros((nx, ROWS, lanes), jnp.float32)
        for x in range(nx):
            for comp in range(3):
                stage[k, x, comp : comp + 1, :] = field[x + 1, pl.ds(8 * comp + line, 1), :]
        copies = halo_copies(k, field, rows)
        copies[0].start()

        @pl.when(brick > 0)
        def _():
            copies[1].start()
            copies[2].start()

        @pl.when(brick < last)
        def _():
            copies[3].start()
            copies[4].start()

    def wait_side(k, field, rows):
        halo_copies(k, field, rows)[0].wait()

    def wait_ends(k, field, rows):
        copies = halo_copies(k, field, rows)

        @pl.when(brick > 0)
        def _():
            copies[1].wait_send()
            copies[2].wait_send()
            copies[3].wait_recv()
            copies[4].wait_recv()

        @pl.when(brick < last)
        def _():
            copies[3].wait_send()
            copies[4].wait_send()
            copies[1].wait_recv()
            copies[2].wait_recv()

    def density_copies():
        return (
            remote(dens_ref, dens_side.at[pl.ds(1, nx)], dsend_sem.at[0], drecv_sem.at[0], {"sub": other}),
            remote(dens_ref.at[nx - 1], dens_own.at[0], dsend_sem.at[1], drecv_sem.at[1], upper),
            remote(dens_ref.at[nx - 1], dens_side.at[0], dsend_sem.at[2], drecv_sem.at[2], upper_side),
        )

    def sum_copies(k):
        return [
            remote(sums_out.at[k], sums.at[k, n - 1], psend_sem.at[k, n - 1], precv_sem.at[k, n - 1], peer(n))
            for n in range(1, group)
        ]

    def send_sums(k, parts):
        sums_out[k] = jnp.zeros(sums_out.shape[1:], jnp.float32)
        for q, part in enumerate(parts):
            line = jnp.sum(part, axis=0, keepdims=True)
            for c in range(count):
                row = q * count + c
                sums_out[k, row : row + 1, :] = line[:, c * LANES : (c + 1) * LANES]
        for copy in sum_copies(k):
            copy.start()

    def wait_sums(k):
        for copy in sum_copies(k):
            copy.wait()
        total = sums_out[k]
        for n in range(group - 1):
            total = total + sums[k, n]
        return jnp.sum(total, axis=1, keepdims=True)

    def widen(column):
        return jnp.concatenate(
            [jnp.broadcast_to(column[c : c + 1], (1, LANES)) for c in range(count)], axis=1
        )

    def over_cases(tile):
        return jnp.concatenate([tile] * count, axis=1)

    fetches[0].wait()
    fetches[1].wait()

    for x in range(nx):
        for comp in range(3):
            tile = (1 - mask_ref[comp, x]).astype(jnp.float32)
            free[x, 8 * comp : 8 * comp + 8, :] = tile
            for c in range(count):
                u_f[x + 1, 8 * comp : 8 * comp + 8, c * LANES : (c + 1) * LANES] = (
                    start_ref[c, comp, x] * tile
                )
    no_plane = jnp.zeros((24, lanes), jnp.float32)
    no_rows = jnp.zeros((ROWS, lanes), jnp.float32)
    no_tile = jnp.zeros((ROWS, LANES), jnp.float32)

    @pl.when(brick == 0)
    def _():
        for field in (u_f, d_f, q_f):
            field[0] = no_plane
        for rows in (u_h, d_h, q_h):
            rows[0] = no_rows
        dens_own[0] = no_tile
        dens_side[0] = no_tile

    @pl.when(brick == last)
    def _():
        for field in (u_f, d_f, q_f):
            field[nx + 1] = no_plane
        for rows in (u_h, d_h, q_h):
            rows[nx + 1] = no_rows

    pl.semaphore_wait(barrier, group - 1 + cases - 1)
    send_halo(0, u_f, u_h)
    fetches[2].wait()
    copies = density_copies()
    copies[0].start()

    @pl.when(brick < last)
    def _():
        copies[1].start()
        copies[2].start()

    for fetch in fetches[3:]:
        fetch.wait()
    stiff = stiff_ref[...]
    spread_stiff = exact_dot(stiff, spread_ref[...])
    matrix = keep_ref[0] * exact_dot(pick_ref[0], spread_stiff)
    matrix = matrix + keep_ref[1] * exact_dot(pick_ref[1], spread_stiff)
    m_hi[...], m_lo[...] = split(matrix)
    matrix = None
    for b in (0, 1):
        part = keep3_ref[b] * exact_dot(pick3_ref[...], exact_dot(stiff, spread3_ref[b]))
        matrix = part if matrix is None else matrix + part
    high, low = split(matrix)
    n_hi[...] = high
    n_lo[...] = low

    y_bits = int(total_y).bit_length() - 1
    z_bits = LANES.bit_length() - 1
    load_count = nodes_ref.shape[1]
    for c in range(count):
        node = nodes_ref[c : c + 1, :]
        place_z = node & (LANES - 1)
        place_y = ((node >> z_bits) & (total_y - 1)) - sub * ROWS
        place_x = (node >> (z_bits + y_bits)) - brick * nx
        inside = (place_y >= 0) & (place_y < ROWS) & (place_x >= 0) & (place_x < nx)
        place = jnp.where(inside, place_x * ROWS + place_y, -1)
        hit = lax.broadcasted_iota(jnp.int32, (nx * ROWS, load_count), 0) == place
        depth = lax.broadcasted_iota(jnp.int32, (LANES, load_count), 0) == place_z
        depth = jnp.where(depth, 1.0, 0.0).astype(jnp.bfloat16)
        for comp in range(3):
            force = forces_ref[comp, c : c + 1, :].astype(jnp.float32)
            weighted = jnp.where(hit, force, 0.0).astype(jnp.bfloat16)
            block = lax.dot_general(
                weighted, depth, (((1,), (1,)), ((), ())), preferred_element_type=jnp.float32
            )
            for x in range(nx):
                loads[x, 8 * comp : 8 * comp + 8, c * LANES : (c + 1) * LANES] = block[8 * x : 8 * x + 8]

    density_copies()[0].wait()
    row_number = lax.broadcasted_iota(jnp.int32, (ROWS, LANES), 0)
    dens_own[1 : nx + 1] = dens_ref[...]

    def layer_scale(i):
        def scale_of(density):
            scale = SOFT_FLOOR + (1.0 - SOFT_FLOOR) * (density * density * density)
            return jnp.where(brick > 0, scale, 0.0) if i == 0 else scale

        own = scale_of(dens_own[i])
        below = jnp.where(sub > 0, scale_of(dens_side[i]), 0.0)
        own_edge = jnp.broadcast_to(own[7:8], (ROWS, LANES))
        below_edge = jnp.broadcast_to(below[7:8], (ROWS, LANES))
        s_own[i] = own
        s_shift[i] = jnp.where(row_number == 0, below_edge, pltpu.roll(own, 1, 0))
        s_edge[i] = jnp.where(sub > 0, below_edge, own_edge)

    for i in range(1, nx + 1):
        layer_scale(i)

    def by_case(value, shift, edge):
        parts = []
        for c in range(count):
            part = value[:, c * LANES : (c + 1) * LANES]
            part = pltpu.roll(part, shift, 1)
            at = lax.broadcasted_iota(jnp.int32, part.shape, 1)
            parts.append(jnp.where(at == edge, 0.0, part))
        return jnp.concatenate(parts, axis=1)

    def ahead(value):
        return by_case(value, LANES - 1, LANES - 1)

    def behind(value):
        return by_case(value, 1, 0)

    def prepare(p, field, rows):
        value = field[p]
        edge = rows[p]
        terms[p, 0:24, :] = value
        terms[p, 24:48, :] = ahead(value)
        terms[p, 48:56, :] = edge
        terms[p, 56:64, :] = ahead(edge)

    def layer_forces(i):
        own = over_cases(s_own[i])[None]
        shift = over_cases(s_shift[i])[None]
        edge = over_cases(s_edge[i])[None]
        parts = []
        for a in (0, 1):
            main = terms[i + a, 0:48, :].reshape(6, ROWS, lanes)
            side = terms[i + a, 48:64, :].reshape(2, ROWS, lanes)
            parts += [main * own, main * shift, side * edge]
        high, low = split(jnp.concatenate(parts, axis=0).reshape(224, lanes))
        return dot16(m_hi[...], high) + dot16(m_hi[...], low) + dot16(m_lo[...], high)

    def element_pass(field, rows, ends, take, init):
        prepare(1, field, rows)
        prepare(2, field, rows)
        out = layer_forces(1)
        first[...] = out[0:48]
        before[...] = out[48:96]

        def step(i, carry):
            out = layer_forces(i)
            total = out[0:48] + before[...]
            before[...] = out[48:96]
            return take(i, total[0:24] + behind(total[24:48]), carry)

        def inner(i, carry):
            prepare(i + 1, field, rows)
            return step(i, carry)

        carry = lax.fori_loop(2, nx, inner, init, unroll=UNROLL)
        ends()
        prepare(0, field, rows)
        prepare(nx + 1, field, rows)
        total = first[...] + layer_forces(0)[48:96]
        carry = take(1, total[0:24] + behind(total[24:48]), carry)
        return step(nx, carry)

    def fold(value):
        return value[0:8] + value[8:16] + value[16:24]

    wait_side(0, u_f, u_h)

    def start_ends():
        copies = density_copies()

        @pl.when(brick < last)
        def _():
            copies[1].wait_send()
            copies[2].wait_send()

        @pl.when(brick > 0)
        def _():
            copies[1].wait_recv()
            copies[2].wait_recv()

        layer_scale(0)
        wait_ends(0, u_f, u_h)

    def take_start(i, force, carry):
        residual = (loads[i - 1] - force) * over_cases(free[i - 1])
        d_f[i] = residual
        return carry + fold(residual * residual)

    norm_part = element_pass(u_f, u_h, start_ends, take_start, no_rows)
    send_halo(1, d_f, d_h)
    wait_side(1, d_f, d_h)

    def take_first(i, force, carry):
        image = force * over_cases(free[i - 1])
        q_f[i] = image
        return carry + fold(image * d_f[i])

    inner_part = element_pass(d_f, d_h, lambda: wait_ends(1, d_f, d_h), take_first, no_rows)
    send_halo(2, q_f, q_h)
    send_sums(0, (inner_part, norm_part))
    wait_side(2, q_f, q_h)

    def take_second(i, force, carry):
        g_f[i - 1] = force * over_cases(free[i - 1])
        return carry

    element_pass(q_f, q_h, lambda: wait_ends(2, q_f, q_h), take_second, 0)
    total = wait_sums(0)
    norm_now = total[count : 2 * count]
    inner_now = total[0:count]
    step_length = widen(norm_now / inner_now)
    norm_part = no_rows
    inner_part = no_rows
    cross_part = no_rows
    for x in range(1, nx + 1):
        direction = d_f[x]
        image = q_f[x]
        residual = direction - step_length * image
        residual_image = image - step_length * g_f[x - 1]
        r_f[x] = residual
        norm_part = norm_part + fold(residual * residual)
        inner_part = inner_part + fold(residual * residual_image)
        cross_part = cross_part + fold(residual * image + direction * residual_image)
    send_sums(1, (norm_part, inner_part, cross_part))
    r_f[nx + 1] = d_f[nx + 1] - step_length * q_f[nx + 1]
    for x in range(1, nx + 2):
        r_h[x] = d_h[x] - step_length * q_h[x]
        u_f[x] = u_f[x] + step_length * d_f[x]
        u_h[x] = u_h[x] + step_length * d_h[x]
    total = wait_sums(1)
    norm_next = total[0:count]
    ratio = norm_next / norm_now
    inner = total[count : 2 * count] + ratio * total[2 * count : 3 * count]
    inner = inner + ratio * ratio * inner_now
    step_length = widen(norm_next / inner)
    ratio = widen(ratio)
    for x in range(1, nx + 2):
        moved = u_f[x] + step_length * (r_f[x] + ratio * d_f[x])
        u_f[x] = moved
        u_h[x] = u_h[x] + step_length * (r_h[x] + ratio * d_h[x])
        if x <= nx:
            for c in range(count):
                for comp in range(3):
                    disp_ref[c, comp, x - 1] = moved[
                        8 * comp : 8 * comp + 8, c * LANES : (c + 1) * LANES
                    ]

    weights = [weights_ref[case * count + c].astype(jnp.float32) for c in range(count)]
    wide_rows = lax.broadcasted_iota(jnp.int32, (ROWS, lanes), 0)

    def raised(p):
        edge_on = jnp.where(sub == 0, 1.0, 0.0)
        blocks = []
        for c in (0, 1):
            edge = terms[p, 48 + 8 * c : 56 + 8 * c, :] * edge_on
            for comp in range(3):
                start = 24 * c + 8 * comp
                block = pltpu.roll(terms[p, start : start + 8, :], 7, 0)
                blocks.append(jnp.where(wide_rows == 7, edge[comp : comp + 1], block))
        return jnp.concatenate(blocks, axis=0)

    prepare(1, u_f, u_h)

    def energy_step(i, carry):
        prepare(i + 1, u_f, u_h)
        both = terms[pl.ds(i, 2)].reshape(128, lanes)
        high, low = split(both)
        out = dot16(n_hi[...], high) + dot16(n_hi[...], low) + dot16(n_lo[...], high)
        found = no_rows
        for a in (0, 1):
            for b in (0, 1):
                value = raised(i + a) if b else terms[i + a, 0:48, :]
                base = 96 * a + 48 * b
                product = (value * out[base : base + 48]).reshape(6, ROWS, lanes)
                found = found + jnp.sum(product, axis=0)
        weighted = no_tile
        for c in range(count):
            weighted = weighted + weights[c] * found[:, c * LANES : (c + 1) * LANES]
        energy[i - 1] = weighted
        return carry

    lax.fori_loop(1, nx + 1, energy_step, 0, unroll=ENERGY_UNROLL)

    copies = [
        remote(energy, energy_in.at[n - 1], esend_sem.at[n - 1], erecv_sem.at[n - 1], case_peer(n))
        for n in range(1, cases)
    ]
    for copy in copies:
        copy.start()
    for copy in copies:
        copy.wait()
    weight_sum = weights_ref[0].astype(jnp.float32)
    for n in range(1, weights_ref.shape[0]):
        weight_sum = weight_sum + weights_ref[n].astype(jnp.float32)
    share = LANES // cases
    for x in range(nx):
        total = energy[x]
        for n in range(cases - 1):
            total = total + energy_in[n, x]
        density = dens_ref[x]
        result = -(PENALTY * (1.0 - SOFT_FLOOR)) * (density * density) * total / weight_sum
        owned = result[:, 0:share]
        for n in range(1, cases):
            owned = jnp.where(case == n, result[:, n * share : (n + 1) * share], owned)
        sens_ref[x] = owned


def per_device(
    mesh_shape, densities, fixed_mask, start_field, load_nodes, load_forces, case_weights, stiffness
):
    bricks, cases = mesh_shape["brick"], mesh_shape["case"]
    assert mesh_shape["sub"] == 2
    count, _, nx, ny, nz = start_field.shape
    assert ny == ROWS and nz == LANES
    lanes = count * LANES
    group = 2 * bricks
    sum_rows = -(-3 * count // 8) * 8
    pick, spread, keep = force_constants()
    pick3, spread3, keep3 = energy_constants()
    f32, bf16 = jnp.float32, jnp.bfloat16
    vmem = pl.BlockSpec(memory_space=pltpu.VMEM)
    dma = pltpu.SemaphoreType.DMA
    plane = pltpu.VMEM((nx + 2, 24, lanes), f32)
    rows = pltpu.VMEM((nx + 2, ROWS, lanes), f32)
    scales = pltpu.VMEM((nx + 1, ROWS, LANES), f32)
    arguments = (
        densities, fixed_mask, start_field, load_nodes, jnp.transpose(load_forces, (2, 0, 1)),
        case_weights, stiffness,
    )
    return pl.pallas_call(
        functools.partial(kernel, (bricks, cases, count, nx, 2 * ROWS)),
        out_shape=(
            jax.ShapeDtypeStruct(start_field.shape, f32),
            jax.ShapeDtypeStruct((nx, ROWS, LANES // cases), f32),
        ),
        in_specs=[pl.BlockSpec(memory_space=pltpu.HBM)] * 13,
        out_specs=(vmem, vmem),
        scratch_shapes=[
            *(pltpu.VMEM(x.shape, x.dtype) for x in arguments[:5]),
            pltpu.SMEM(case_weights.shape, case_weights.dtype),
            pltpu.VMEM(stiffness.shape, f32),
            pltpu.VMEM(pick.shape, f32), pltpu.VMEM(spread.shape[1:], f32),
            pltpu.VMEM(keep.shape[1:], f32),
            pltpu.VMEM(pick3.shape, f32), pltpu.VMEM(spread3.shape, f32),
            pltpu.VMEM(keep3.shape[1:], f32),
            dma((13,)), pltpu.VMEM((48, lanes), f32),
            plane, plane, plane, plane,
            pltpu.VMEM((nx, 24, lanes), f32),
            rows, rows, rows, rows,
            pltpu.VMEM((3, nx, ROWS, lanes), f32),
            pltpu.VMEM((nx + 2, 64, lanes), f32),
            pltpu.VMEM((48, lanes), f32),
            pltpu.VMEM((nx, 24, lanes), f32),
            pltpu.VMEM((nx, 24, LANES), f32),
            scales, scales, scales, scales, scales,
            pltpu.VMEM((96, 224), bf16),
            pltpu.VMEM((96, 224), bf16),
            pltpu.VMEM((192, 128), bf16),
            pltpu.VMEM((192, 128), bf16),
            pltpu.VMEM((3, group - 1, sum_rows, LANES), f32),
            pltpu.VMEM((3, sum_rows, LANES), f32),
            pltpu.VMEM((nx, ROWS, LANES), f32),
            pltpu.VMEM((max(cases - 1, 1), nx, ROWS, LANES), f32),
            dma((3, 5)), dma((3, 5)), dma((3,)), dma((3,)),
            dma((3, group - 1)), dma((3, group - 1)),
            dma((max(cases - 1, 1),)), dma((max(cases - 1, 1),)),
        ],
        compiler_params=pltpu.CompilerParams(
            collective_id=0, has_side_effects=True, vmem_limit_bytes=VMEM_BYTES
        ),
    )(*arguments, *(jnp.asarray(x) for x in (pick, spread, keep, pick3, spread3, keep3)))


def solution(mesh):
    return jax.shard_map(
        functools.partial(per_device, dict(mesh.shape)),
        mesh=mesh,
        in_specs=(
            P(("design", "brick"), "sub", None),
            P(None, ("design", "brick"), "sub", None),
            P("case", None, ("design", "brick"), "sub", None),
            P("case", None),
            P("case", None, None),
            P(),
            P(),
        ),
        out_specs=(
            P("case", None, ("design", "brick"), "sub", None),
            P(("design", "brick"), "sub", "case"),
        ),
        check_vma=False,
    )
```

```python
import functools

import jax
import jax.numpy as jnp
import numpy as np
from jax import lax
from jax.experimental import pallas as pl
from jax.experimental.pallas import tpu as pltpu
from jax.sharding import PartitionSpec as P

PENALTY = 3.0
SOFT_FLOOR = 0.001
MESH = pl.DeviceIdType.MESH
UNROLL = 6
ENERGY_UNROLL = 8
VMEM_BYTES = 63 * 2**20 + 2**19
ROWS = 8
LANES = 128


def corner_index(a, b, c, comp):
    return 3 * (4 * a + 2 * b + c) + comp


def force_constants():
    pick = np.zeros((2, 96, 24), np.float32)
    spread = np.zeros((2, 24, 224), np.float32)
    keep = np.zeros((2, 2, 96, 224), np.float32)
    rows = []
    for a in (0, 1):
        for c in (0, 1):
            for comp in range(3):
                for y in range(ROWS):
                    for b in (0, 1):
                        pick[b, len(rows), corner_index(a, b, c, comp)] = 1
                    rows.append(y)
    for side in (0, 1):
        columns = []
        for a in (0, 1):
            for b in (0, 1):
                for c in (0, 1):
                    for comp in range(3):
                        for y in range(ROWS):
                            columns.append((corner_index(a, b, c, comp), y - b))
            for c in (0, 1):
                for comp in range(ROWS):
                    if comp < 3:
                        b = 1 - side
                        columns.append((corner_index(a, b, c, comp), 7 if side == 0 else -1))
                    else:
                        columns.append(None)
        for n, column in enumerate(columns):
            if column is None:
                continue
            spread[side, column[0], n] = 1
            for m, y in enumerate(rows):
                if y - column[1] in (0, 1):
                    keep[side, y - column[1], m, n] = 1
    return pick, spread, keep


def energy_constants():
    pick = np.zeros((192, 24), np.float32)
    spread = np.zeros((2, 24, 128), np.float32)
    keep = np.zeros((2, 2, 192, 128), np.float32)
    for j in range(24):
        pick[8 * j : 8 * j + 8, j] = 1
    for side in (0, 1):
        for a in (0, 1):
            for c in (0, 1):
                for comp in range(3):
                    for b in (0, 1):
                        for y in range(ROWS):
                            n = 64 * a + 24 * c + 8 * comp + y
                            spread[b, corner_index(a, b, c, comp), n] = 1
                            if y - b >= 0:
                                keep[side, b, y - b :: 8, n] = 1
                        n = 64 * a + 48 + 8 * c + comp
                        spread[b, corner_index(a, b, c, comp), n] = 1
                        if side == 0 and b == 1:
                            keep[side, b, 7::8, n] = 1
    return pick, spread, keep


def split(value):
    high = value.astype(jnp.bfloat16)
    return high, (value - high.astype(jnp.float32)).astype(jnp.bfloat16)


def exact_dot(a, b):
    return jnp.dot(a, b, precision=lax.Precision.HIGHEST, preferred_element_type=jnp.float32)


def dot16(a, b):
    return jnp.dot(a, b, preferred_element_type=jnp.float32)


def kernel(
    sizes,
    dens_hbm, mask_hbm, start_hbm, nodes_hbm, forces_hbm, weights_hbm, stiff_hbm,
    pick_hbm, spread_hbm, keep_hbm, pick3_hbm, spread3_hbm, keep3_hbm,
    disp_hbm, sens_ref,
    dens_ref, mask_ref, start_ref, nodes_ref, forces_ref, weights_ref, stiff_ref,
    pick_ref, spread_ref, keep_ref, pick3_ref, spread3_ref, keep3_ref, load_sem, first, disp_ref, out_sem,
    u_f, d_f, q_f, r_f, g_f, u_h, d_h, q_h, r_h, stage,
    terms, before, loads, free, dens_own, dens_side, s_own, s_shift, s_edge,
    m_hi, m_lo, n_hi, n_lo, sums, sums_out, energy, energy_in,
    send_sem, recv_sem, dsend_sem, drecv_sem, psend_sem, precv_sem, esend_sem, erecv_sem,
):
    bricks, cases, count, nx, total_y = sizes
    lanes = count * LANES
    brick = lax.axis_index("brick")
    sub = lax.axis_index("sub")
    case = lax.axis_index("case")
    group = 2 * bricks
    me = 2 * brick + sub
    last = bricks - 1
    other = 1 - sub

    def peer(k):
        target = lax.rem(me + k, group)
        return {"brick": target // 2, "sub": lax.rem(target, 2)}

    def case_peer(k):
        return {"case": lax.rem(case + k, cases)}

    inputs = (
        (start_hbm, start_ref), (mask_hbm, mask_ref), (dens_hbm, dens_ref),
        (stiff_hbm, stiff_ref), (spread_hbm.at[sub], spread_ref), (pick_hbm, pick_ref),
        (keep_hbm.at[sub], keep_ref), (spread3_hbm, spread3_ref), (pick3_hbm, pick3_ref),
        (keep3_hbm.at[sub], keep3_ref), (nodes_hbm, nodes_ref), (forces_hbm, forces_ref),
        (weights_hbm, weights_ref),
    )
    fetches = [
        pltpu.make_async_copy(src, dst, load_sem.at[n]) for n, (src, dst) in enumerate(inputs)
    ]
    barrier = pltpu.get_barrier_semaphore()
    for k in range(1, group):
        pl.semaphore_signal(barrier, inc=1, device_id=peer(k), device_id_type=MESH)
    for k in range(1, cases):
        pl.semaphore_signal(barrier, inc=1, device_id=case_peer(k), device_id_type=MESH)

    for fetch in fetches:
        fetch.start()

    def remote(src, dst, send, recv, device):
        return pltpu.make_async_remote_copy(
            src_ref=src, dst_ref=dst, send_sem=send, recv_sem=recv,
            device_id=device, device_id_type=MESH,
        )

    lower = {"brick": brick - 1}
    upper = {"brick": brick + 1}
    lower_side = {"brick": brick - 1, "sub": other}
    upper_side = {"brick": brick + 1, "sub": other}

    def halo_copies(k, field, rows):
        def sems(n):
            return send_sem.at[k, n], recv_sem.at[k, n]

        return (
            remote(stage.at[k], rows.at[pl.ds(1, nx)], *sems(0), {"sub": other}),
            remote(field.at[1], field.at[nx + 1], *sems(1), lower),
            remote(stage.at[k, 0], rows.at[nx + 1], *sems(2), lower_side),
            remote(field.at[nx], field.at[0], *sems(3), upper),
            remote(stage.at[k, nx - 1], rows.at[0], *sems(4), upper_side),
        )

    def send_halo(k, field, rows):
        line = 7 * (1 - sub)
        copies = halo_copies(k, field, rows)

        @pl.when(brick > 0)
        def _():
            copies[1].start()

        @pl.when(brick < last)
        def _():
            copies[3].start()

        for x in range(nx):
            for comp in range(3):
                stage[k, x, comp : comp + 1, :] = field[x + 1, pl.ds(8 * comp + line, 1), :]
        copies[0].start()

        @pl.when(brick > 0)
        def _():
            copies[2].start()

        @pl.when(brick < last)
        def _():
            copies[4].start()

    def wait_side(k, field, rows):
        halo_copies(k, field, rows)[0].wait()

    def wait_ends(k, field, rows):
        copies = halo_copies(k, field, rows)

        @pl.when(brick > 0)
        def _():
            copies[1].wait_send()
            copies[2].wait_send()
            copies[3].wait_recv()
            copies[4].wait_recv()

        @pl.when(brick < last)
        def _():
            copies[3].wait_send()
            copies[4].wait_send()
            copies[1].wait_recv()
            copies[2].wait_recv()

    def density_copies():
        return (
            remote(dens_ref, dens_side.at[pl.ds(1, nx)], dsend_sem.at[0], drecv_sem.at[0], {"sub": other}),
            remote(dens_ref.at[nx - 1], dens_own.at[0], dsend_sem.at[1], drecv_sem.at[1], upper),
            remote(dens_ref.at[nx - 1], dens_side.at[0], dsend_sem.at[2], drecv_sem.at[2], upper_side),
        )

    def sum_copies(k):
        return [
            remote(sums_out.at[k], sums.at[k, n - 1], psend_sem.at[k, n - 1], precv_sem.at[k, n - 1], peer(n))
            for n in range(1, group)
        ]

    def send_sums(k, parts):
        sums_out[k] = jnp.zeros(sums_out.shape[1:], jnp.float32)
        for q, part in enumerate(parts):
            line = jnp.sum(part, axis=0, keepdims=True)
            for c in range(count):
                row = q * count + c
                sums_out[k, row : row + 1, :] = line[:, c * LANES : (c + 1) * LANES]
        for copy in sum_copies(k):
            copy.start()

    def wait_sums(k):
        for copy in sum_copies(k):
            copy.wait()
        total = sums_out[k]
        for n in range(group - 1):
            total = total + sums[k, n]
        return jnp.sum(total, axis=1, keepdims=True)

    def widen(column):
        return jnp.concatenate(
            [jnp.broadcast_to(column[c : c + 1], (1, LANES)) for c in range(count)], axis=1
        )

    def over_cases(tile):
        return jnp.concatenate([tile] * count, axis=1)

    stage[...] = jnp.zeros(stage.shape, jnp.float32)
    fetches[0].wait()
    fetches[1].wait()

    for x in range(nx):
        for comp in range(3):
            tile = (1 - mask_ref[comp, x]).astype(jnp.float32)
            free[x, 8 * comp : 8 * comp + 8, :] = tile
            for c in range(count):
                u_f[x + 1, 8 * comp : 8 * comp + 8, c * LANES : (c + 1) * LANES] = (
                    start_ref[c, comp, x] * tile
                )
    no_plane = jnp.zeros((24, lanes), jnp.float32)
    no_rows = jnp.zeros((ROWS, lanes), jnp.float32)
    no_tile = jnp.zeros((ROWS, LANES), jnp.float32)

    @pl.when(brick == 0)
    def _():
        for field in (u_f, d_f, q_f):
            field[0] = no_plane
        for rows in (u_h, d_h, q_h):
            rows[0] = no_rows
        dens_own[0] = no_tile
        dens_side[0] = no_tile

    @pl.when(brick == last)
    def _():
        for field in (u_f, d_f, q_f):
            field[nx + 1] = no_plane
        for rows in (u_h, d_h, q_h):
            rows[nx + 1] = no_rows

    pl.semaphore_wait(barrier, group - 1 + cases - 1)
    send_halo(0, u_f, u_h)
    fetches[2].wait()
    copies = density_copies()
    copies[0].start()

    @pl.when(brick < last)
    def _():
        copies[1].start()
        copies[2].start()

    for fetch in fetches[3:]:
        fetch.wait()
    stiff = stiff_ref[...]
    spread_stiff = exact_dot(stiff, spread_ref[...])
    matrix = keep_ref[0] * exact_dot(pick_ref[0], spread_stiff)
    matrix = matrix + keep_ref[1] * exact_dot(pick_ref[1], spread_stiff)
    m_hi[...], m_lo[...] = split(matrix)
    matrix = None
    for b in (0, 1):
        part = keep3_ref[b] * exact_dot(pick3_ref[...], exact_dot(stiff, spread3_ref[b]))
        matrix = part if matrix is None else matrix + part
    high, low = split(matrix)
    n_hi[...] = high
    n_lo[...] = low

    y_bits = int(total_y).bit_length() - 1
    z_bits = LANES.bit_length() - 1
    load_count = nodes_ref.shape[1]
    for c in range(count):
        node = nodes_ref[c : c + 1, :]
        place_z = node & (LANES - 1)
        place_y = ((node >> z_bits) & (total_y - 1)) - sub * ROWS
        place_x = (node >> (z_bits + y_bits)) - brick * nx
        inside = (place_y >= 0) & (place_y < ROWS) & (place_x >= 0) & (place_x < nx)
        place = jnp.where(inside, place_x * ROWS + place_y, -1)
        hit = lax.broadcasted_iota(jnp.int32, (nx * ROWS, load_count), 0) == place
        depth = lax.broadcasted_iota(jnp.int32, (LANES, load_count), 0) == place_z
        depth = jnp.where(depth, 1.0, 0.0).astype(jnp.bfloat16)
        for comp in range(3):
            force = forces_ref[comp, c : c + 1, :].astype(jnp.float32)
            weighted = jnp.where(hit, force, 0.0).astype(jnp.bfloat16)
            block = lax.dot_general(
                weighted, depth, (((1,), (1,)), ((), ())), preferred_element_type=jnp.float32
            )
            for x in range(nx):
                loads[x, 8 * comp : 8 * comp + 8, c * LANES : (c + 1) * LANES] = block[8 * x : 8 * x + 8]

    density_copies()[0].wait()
    row_number = lax.broadcasted_iota(jnp.int32, (ROWS, LANES), 0)
    dens_own[1 : nx + 1] = dens_ref[...]

    def layer_scale(i):
        def scale_of(density):
            scale = SOFT_FLOOR + (1.0 - SOFT_FLOOR) * (density * density * density)
            return jnp.where(brick > 0, scale, 0.0) if i == 0 else scale

        own = scale_of(dens_own[i])
        below = jnp.where(sub > 0, scale_of(dens_side[i]), 0.0)
        own_edge = jnp.broadcast_to(own[7:8], (ROWS, LANES))
        below_edge = jnp.broadcast_to(below[7:8], (ROWS, LANES))
        s_own[i] = own
        s_shift[i] = jnp.where(row_number == 0, below_edge, pltpu.roll(own, 1, 0))
        s_edge[i] = jnp.where(sub > 0, below_edge, own_edge)

    for i in range(1, nx + 1):
        layer_scale(i)

    def by_case(value, shift, edge):
        parts = []
        for c in range(count):
            part = value[:, c * LANES : (c + 1) * LANES]
            part = pltpu.roll(part, shift, 1)
            at = lax.broadcasted_iota(jnp.int32, part.shape, 1)
            parts.append(jnp.where(at == edge, 0.0, part))
        return jnp.concatenate(parts, axis=1)

    def ahead(value):
        return by_case(value, LANES - 1, LANES - 1)

    def behind(value):
        return by_case(value, 1, 0)

    def prepare(p, field, rows):
        value = field[p]
        edge = rows[p]
        terms[p, 0:24, :] = value
        terms[p, 24:48, :] = ahead(value)
        terms[p, 48:56, :] = edge
        terms[p, 56:64, :] = ahead(edge)

    def layer_forces(i):
        own = over_cases(s_own[i])[None]
        shift = over_cases(s_shift[i])[None]
        edge = over_cases(s_edge[i])[None]
        parts = []
        for a in (0, 1):
            main = terms[i + a, 0:48, :].reshape(6, ROWS, lanes)
            side = terms[i + a, 48:64, :].reshape(2, ROWS, lanes)
            parts += [main * own, main * shift, side * edge]
        high, low = split(jnp.concatenate(parts, axis=0).reshape(224, lanes))
        return dot16(m_hi[...], high) + dot16(m_hi[...], low) + dot16(m_lo[...], high)

    def element_pass(field, rows, ends, take, init):
        prepare(1, field, rows)
        prepare(2, field, rows)
        out = layer_forces(1)
        first[...] = out[0:48]
        before[...] = out[48:96]

        def step(i, carry):
            out = layer_forces(i)
            total = out[0:48] + before[...]
            before[...] = out[48:96]
            return take(i, total[0:24] + behind(total[24:48]), carry)

        def inner(i, carry):
            prepare(i + 1, field, rows)
            return step(i, carry)

        carry = lax.fori_loop(2, nx, inner, init, unroll=UNROLL)
        ends()
        prepare(0, field, rows)
        prepare(nx + 1, field, rows)
        total = first[...] + layer_forces(0)[48:96]
        carry = take(1, total[0:24] + behind(total[24:48]), carry)
        return step(nx, carry)

    def fold(value):
        return value[0:8] + value[8:16] + value[16:24]

    wait_side(0, u_f, u_h)

    def start_ends():
        copies = density_copies()

        @pl.when(brick < last)
        def _():
            copies[1].wait_send()
            copies[2].wait_send()

        @pl.when(brick > 0)
        def _():
            copies[1].wait_recv()
            copies[2].wait_recv()

        layer_scale(0)
        wait_ends(0, u_f, u_h)

    def take_start(i, force, carry):
        residual = (loads[i - 1] - force) * over_cases(free[i - 1])
        d_f[i] = residual
        return carry + fold(residual * residual)

    norm_part = element_pass(u_f, u_h, start_ends, take_start, no_rows)
    send_halo(1, d_f, d_h)
    wait_side(1, d_f, d_h)

    def take_first(i, force, carry):
        image = force * over_cases(free[i - 1])
        q_f[i] = image
        return carry + fold(image * d_f[i])

    inner_part = element_pass(d_f, d_h, lambda: wait_ends(1, d_f, d_h), take_first, no_rows)
    send_halo(2, q_f, q_h)
    send_sums(0, (inner_part, norm_part))
    wait_side(2, q_f, q_h)

    def take_second(i, force, carry):
        g_f[i - 1] = force * over_cases(free[i - 1])
        return carry

    element_pass(q_f, q_h, lambda: wait_ends(2, q_f, q_h), take_second, 0)
    total = wait_sums(0)
    norm_now = total[count : 2 * count]
    inner_now = total[0:count]
    step_length = widen(norm_now / inner_now)
    norm_part = no_rows
    inner_part = no_rows
    cross_part = no_rows
    for x in range(1, nx + 1):
        direction = d_f[x]
        image = q_f[x]
        residual = direction - step_length * image
        residual_image = image - step_length * g_f[x - 1]
        r_f[x] = residual
        norm_part = norm_part + fold(residual * residual)
        inner_part = inner_part + fold(residual * residual_image)
        cross_part = cross_part + fold(residual * image + direction * residual_image)
    send_sums(1, (norm_part, inner_part, cross_part))
    r_f[nx + 1] = d_f[nx + 1] - step_length * q_f[nx + 1]
    for x in range(1, nx + 2):
        r_h[x] = d_h[x] - step_length * q_h[x]
        u_f[x] = u_f[x] + step_length * d_f[x]
        u_h[x] = u_h[x] + step_length * d_h[x]
    total = wait_sums(1)
    norm_next = total[0:count]
    ratio = norm_next / norm_now
    inner = total[count : 2 * count] + ratio * total[2 * count : 3 * count]
    inner = inner + ratio * ratio * inner_now
    step_length = widen(norm_next / inner)
    ratio = widen(ratio)
    for x in range(1, nx + 2):
        moved = u_f[x] + step_length * (r_f[x] + ratio * d_f[x])
        u_f[x] = moved
        u_h[x] = u_h[x] + step_length * (r_h[x] + ratio * d_h[x])
        if x <= nx:
            for c in range(count):
                for comp in range(3):
                    disp_ref[c, comp, x - 1] = moved[
                        8 * comp : 8 * comp + 8, c * LANES : (c + 1) * LANES
                    ]

    leave = pltpu.make_async_copy(disp_ref, disp_hbm, out_sem)
    leave.start()

    weights = [weights_ref[case * count + c].astype(jnp.float32) for c in range(count)]
    wide_rows = lax.broadcasted_iota(jnp.int32, (ROWS, lanes), 0)

    def raised(p):
        edge_on = jnp.where(sub == 0, 1.0, 0.0)
        blocks = []
        for c in (0, 1):
            edge = terms[p, 48 + 8 * c : 56 + 8 * c, :] * edge_on
            for comp in range(3):
                start = 24 * c + 8 * comp
                block = pltpu.roll(terms[p, start : start + 8, :], 7, 0)
                blocks.append(jnp.where(wide_rows == 7, edge[comp : comp + 1], block))
        return jnp.concatenate(blocks, axis=0)

    prepare(1, u_f, u_h)

    def energy_step(i, carry):
        prepare(i + 1, u_f, u_h)
        both = terms[pl.ds(i, 2)].reshape(128, lanes)
        high, low = split(both)
        out = dot16(n_hi[...], high) + dot16(n_hi[...], low) + dot16(n_lo[...], high)
        found = no_rows
        for a in (0, 1):
            for b in (0, 1):
                value = raised(i + a) if b else terms[i + a, 0:48, :]
                base = 96 * a + 48 * b
                product = (value * out[base : base + 48]).reshape(6, ROWS, lanes)
                found = found + jnp.sum(product, axis=0)
        weighted = no_tile
        for c in range(count):
            weighted = weighted + weights[c] * found[:, c * LANES : (c + 1) * LANES]
        energy[i - 1] = weighted
        return carry

    lax.fori_loop(1, nx + 1, energy_step, 0, unroll=ENERGY_UNROLL)

    copies = [
        remote(energy, energy_in.at[n - 1], esend_sem.at[n - 1], erecv_sem.at[n - 1], case_peer(n))
        for n in range(1, cases)
    ]
    for copy in copies:
        copy.start()
    for copy in copies:
        copy.wait()
    weight_sum = weights_ref[0].astype(jnp.float32)
    for n in range(1, weights_ref.shape[0]):
        weight_sum = weight_sum + weights_ref[n].astype(jnp.float32)
    share = LANES // cases
    for x in range(nx):
        total = energy[x]
        for n in range(cases - 1):
            total = total + energy_in[n, x]
        density = dens_ref[x]
        result = -(PENALTY * (1.0 - SOFT_FLOOR)) * (density * density) * total / weight_sum
        owned = result[:, 0:share]
        for n in range(1, cases):
            owned = jnp.where(case == n, result[:, n * share : (n + 1) * share], owned)
        sens_ref[x] = owned
    leave.wait()


def per_device(
    mesh_shape, densities, fixed_mask, start_field, load_nodes, load_forces, case_weights, stiffness
):
    bricks, cases = mesh_shape["brick"], mesh_shape["case"]
    assert mesh_shape["sub"] == 2
    count, _, nx, ny, nz = start_field.shape
    assert ny == ROWS and nz == LANES
    lanes = count * LANES
    group = 2 * bricks
    sum_rows = -(-3 * count // 8) * 8
    pick, spread, keep = force_constants()
    pick3, spread3, keep3 = energy_constants()
    f32, bf16 = jnp.float32, jnp.bfloat16
    vmem = pl.BlockSpec(memory_space=pltpu.VMEM)
    dma = pltpu.SemaphoreType.DMA
    plane = pltpu.VMEM((nx + 2, 24, lanes), f32)
    rows = pltpu.VMEM((nx + 2, ROWS, lanes), f32)
    scales = pltpu.VMEM((nx + 1, ROWS, LANES), f32)
    arguments = (
        densities, fixed_mask, start_field, load_nodes, jnp.transpose(load_forces, (2, 0, 1)),
        case_weights, stiffness,
    )
    return pl.pallas_call(
        functools.partial(kernel, (bricks, cases, count, nx, 2 * ROWS)),
        out_shape=(
            jax.ShapeDtypeStruct(start_field.shape, f32),
            jax.ShapeDtypeStruct((nx, ROWS, LANES // cases), f32),
        ),
        in_specs=[pl.BlockSpec(memory_space=pltpu.HBM)] * 13,
        out_specs=(pl.BlockSpec(memory_space=pltpu.HBM), vmem),
        scratch_shapes=[
            *(pltpu.VMEM(x.shape, x.dtype) for x in arguments[:5]),
            pltpu.SMEM(case_weights.shape, case_weights.dtype),
            pltpu.VMEM(stiffness.shape, f32),
            pltpu.VMEM(pick.shape, f32), pltpu.VMEM(spread.shape[1:], f32),
            pltpu.VMEM(keep.shape[1:], f32),
            pltpu.VMEM(pick3.shape, f32), pltpu.VMEM(spread3.shape, f32),
            pltpu.VMEM(keep3.shape[1:], f32),
            dma((13,)), pltpu.VMEM((48, lanes), f32),
            pltpu.VMEM(start_field.shape, f32), dma(()),
            plane, plane, plane, plane,
            pltpu.VMEM((nx, 24, lanes), f32),
            rows, rows, rows, rows,
            pltpu.VMEM((3, nx, ROWS, lanes), f32),
            pltpu.VMEM((nx + 2, 64, lanes), f32),
            pltpu.VMEM((48, lanes), f32),
            pltpu.VMEM((nx, 24, lanes), f32),
            pltpu.VMEM((nx, 24, LANES), f32),
            scales, scales, scales, scales, scales,
            pltpu.VMEM((96, 224), bf16),
            pltpu.VMEM((96, 224), bf16),
            pltpu.VMEM((192, 128), bf16),
            pltpu.VMEM((192, 128), bf16),
            pltpu.VMEM((3, group - 1, sum_rows, LANES), f32),
            pltpu.VMEM((3, sum_rows, LANES), f32),
            pltpu.VMEM((nx, ROWS, LANES), f32),
            pltpu.VMEM((max(cases - 1, 1), nx, ROWS, LANES), f32),
            dma((3, 5)), dma((3, 5)), dma((3,)), dma((3,)),
            dma((3, group - 1)), dma((3, group - 1)),
            dma((max(cases - 1, 1),)), dma((max(cases - 1, 1),)),
        ],
        compiler_params=pltpu.CompilerParams(
            collective_id=0, has_side_effects=True, vmem_limit_bytes=VMEM_BYTES
        ),
    )(*arguments, *(jnp.asarray(x) for x in (pick, spread, keep, pick3, spread3, keep3)))


def solution(mesh):
    return jax.shard_map(
        functools.partial(per_device, dict(mesh.shape)),
        mesh=mesh,
        in_specs=(
            P(("design", "brick"), "sub", None),
            P(None, ("design", "brick"), "sub", None),
            P("case", None, ("design", "brick"), "sub", None),
            P("case", None),
            P("case", None, None),
            P(),
            P(),
        ),
        out_specs=(
            P("case", None, ("design", "brick"), "sub", None),
            P(("design", "brick"), "sub", "case"),
        ),
        check_vma=False,
    )
```
